768 devices in a mesh: gx: 16 (over x, y_hi, core), yz: 48 (over z, y_lo).
Axes of the slice: x: 4, y: 8 (y_hi: 2, y_lo: 4; y = y_hi * 4 + y_lo), z: 12, core: 2. Of those that a mesh axis runs over, the one named last changes fastest.
Arguments:
- positions: float32 [16, 48, 3, 64], P('gx', 'yz'), may hold values from 0 to 3
- species: int32 [16, 48, 64], P('gx', 'yz'), may hold values from 0 to 5
- charges: float32 [16, 48, 64], P('gx', 'yz'), may hold values from -1 to 1
- neighbours: int32 [16, 48, 16, 64], P('gx', 'yz'), may hold values from 0 to 567, as said below
- counts: int32 [16, 48, 64], P('gx', 'yz'), may hold values from 4 to 16
- send_list: int32 [16, 48, 56], P('gx', 'yz'), may hold values from 0 to 63, as said below
- species_table: float32 [6, 128], replicated, may hold values from -6 to 6
- charge_weight: float32 [128], replicated, may hold values from -6 to 6
- w_center: bfloat16 [128, 128], replicated, may hold values from -0.5 to 0.5
- w_neigh: bfloat16 [128, 128], replicated, may hold values from -0.5 to 0.5
- w_radial: float32 [8, 128], replicated, may hold values from -4 to 4
- w_two: bfloat16 [128, 128], replicated, may hold values from -0.5 to 0.5
- w_env: bfloat16 [1, 128, 64], replicated, may hold values from -0.5 to 0.5
- w_tensor: bfloat16 [1, 128, 64], replicated, may hold values from -0.5 to 0.5
- w_latent: bfloat16 [1, 320, 128], replicated, may hold values from -0.3125 to 0.3125
- w_out: bfloat16 [128], replicated, may hold values from -0.5 to 0.5
Outputs:
- atom_energy: float32 [16, 48, 64], P('gx', 'yz')
- forces: float32 [16, 48, 3, 64], P('gx', 'yz')
The draws below stay inside these ranges and needn't reach their ends.
Inputs may be any that keep to these rules, and one draw needn't show every extreme that they name: `neighbours`: an entry below 64 names another owned atom, never the atom itself; an entry n of 64 or more names a boundary-set atom of a neighbouring domain as in the reference program, never with b = 4. `send_list`: 56 distinct owned atoms of each domain.
All inputs are finite; a program needn't handle non-finite values.
Results may differ from the reference program's by a relative error of at most 0.013.
Values may be sent and summed in bfloat16 or wider, within the bound.
No kernel may reach another device: no remote copies, remote signals or barrier semaphores. Data moves between devices by JAX's collectives and lax.ppermute only.
A program may use at most 32 MiB of HBM per device.

```python
import jax
import jax.numpy as jnp
from jax import lax

WIDTH = 128
CHANNELS = 64
SPECIES = 6
BASIS = 8
NEIGH = 16
LAYERS = 1
ATOMS = 64
GHOSTS = 56
SLABS = 16
COLUMNS = 48


def draw_neighbours(key, part):
    key = jax.random.fold_in(key, 11)
    slot_total = ATOMS - 1 + 8 * GHOSTS
    drawn = jax.random.randint(key, (SLABS, COLUMNS, NEIGH, ATOMS), 0, slot_total)
    atom_index = jnp.arange(ATOMS).astype(jnp.int32)[None, None, None, :]
    own_index = drawn + (drawn >= atom_index).astype(jnp.int32)
    ghost_index = drawn - (ATOMS - 1)
    block_index = ghost_index // GHOSTS
    block_index = block_index + (block_index >= 4).astype(jnp.int32)
    far_index = ATOMS + block_index * GHOSTS + ghost_index % GHOSTS
    return jnp.where(drawn < ATOMS - 1, own_index, far_index).astype(jnp.int32)


def draw_send_list(key, part):
    key = jax.random.fold_in(key, 23)
    scores = jax.random.randint(key, (SLABS, COLUMNS, ATOMS), 0, 1 << 20)
    distinct = scores * ATOMS + jnp.arange(ATOMS).astype(jnp.int32)[None, None, :]
    order = jnp.argsort(distinct, axis=-1, stable=True)
    return order[:, :, :GHOSTS].astype(jnp.int32)


def plant(values, stream_key, low, high):
    place = [jax.random.randint(jax.random.fold_in(stream_key, axis), (), 0, length) for axis, length in enumerate(values.shape)]
    widest = values.shape.index(max(values.shape))
    next_to = place[:widest] + [(place[widest] + 1) % values.shape[widest]] + place[widest + 1:]
    return values.at[tuple(place)].set(low).at[tuple(next_to)].set(high)


def level_of(rng, shape, cuts, low, top_value):
    def one(dim, shards_of):
        steps = jax.random.uniform(jax.random.fold_in(jax.random.fold_in(rng, 6), dim), (shards_of,), jnp.float32, low / len(cuts), top_value / len(cuts))
        return jnp.repeat(jnp.exp(steps), shape[dim] // shards_of).reshape((-1,) + (1,) * (len(shape) - dim - 1))

    level = one(*cuts[0])
    for cut in cuts[1:]:
        level = level * one(*cut)
    return level


def bell_draw(key, dims, scale, limit, held_as=jnp.bfloat16):
    return jnp.clip(scale * jax.random.normal(key, dims, jnp.float32), -limit, limit).astype(held_as)


def setup_inputs(seed: int = 0) -> dict:
    keys = jax.random.split(jax.random.key(seed), 17)
    return {
        "positions": jnp.clip(3.0 * jax.random.uniform(keys[0], (SLABS, COLUMNS, 3, ATOMS), jnp.float32) ** level_of(keys[0], (SLABS, COLUMNS, 3, ATOMS), ((0, 16), (1, 48)), -0.2, 0.2), 0.0, 3.0),
        "species": plant(jax.random.randint(keys[1], (SLABS, COLUMNS, ATOMS), 0, SPECIES), jax.random.fold_in(keys[1], 1), 0, SPECIES - 1).astype(jnp.int32),
        "charges": jnp.clip(jax.random.uniform(keys[2], (SLABS, COLUMNS, ATOMS), jnp.float32, -1.0, 1.0) * level_of(keys[2], (SLABS, COLUMNS, ATOMS), ((0, 16), (1, 48)), -0.4, 0.0), -1.0, 1.0),
        "neighbours": draw_neighbours(jax.random.fold_in(keys[16], 71), 0),
        "counts": plant(jax.random.randint(keys[4], (SLABS, COLUMNS, ATOMS), 4, NEIGH + 1), jax.random.fold_in(keys[4], 1), 4, NEIGH).astype(jnp.int32),
        "send_list": draw_send_list(jax.random.fold_in(keys[16], 71), 0),
        "species_table": bell_draw(keys[6], (SPECIES, WIDTH), 1.0, 6.0, jnp.float32),
        "charge_weight": bell_draw(keys[7], (WIDTH,), 1.0, 6.0, jnp.float32),
        "w_center": bell_draw(keys[8], (WIDTH, WIDTH), WIDTH ** -0.5, 0.5),
        "w_neigh": bell_draw(keys[9], (WIDTH, WIDTH), WIDTH ** -0.5, 0.5),
        "w_radial": bell_draw(keys[10], (BASIS, WIDTH), 0.7, 4.0, jnp.float32),
        "w_two": bell_draw(keys[11], (WIDTH, WIDTH), WIDTH ** -0.5, 0.5),
        "w_env": bell_draw(keys[12], (LAYERS, WIDTH, CHANNELS), WIDTH ** -0.5, 0.5),
        "w_tensor": bell_draw(keys[13], (LAYERS, WIDTH, CHANNELS), WIDTH ** -0.5, 0.5),
        "w_latent": bell_draw(keys[14], (LAYERS, WIDTH + 3 * CHANNELS, WIDTH), (WIDTH + 3 * CHANNELS) ** -0.5, 0.3125),
        "w_out": bell_draw(keys[15], (WIDTH,), WIDTH ** -0.5, 0.5),
    }


box_side = 3.0
core_sq = 1.0
env_width = 32.0
basis_width = 0.5

def node_hidden(species_value, charge, species_table, charge_weight):
    kinds = jnp.arange(species_table.shape[0]).astype(species_value.dtype)
    onehot = (species_value[:, None] == kinds[None, :]).astype(species_table.dtype)
    mixed = jnp.dot(onehot, species_table, precision=lax.Precision.HIGHEST) + charge[:, None] * charge_weight[None, :]
    return jax.nn.silu(mixed).astype(jnp.bfloat16)

def gaussian_basis(distance, count):
    centres = 1.0 + jnp.arange(count).astype(distance.dtype)
    spread = distance[:, None] - centres[None, :]
    return jnp.exp(-spread * spread / basis_width)

def harmonics(direction):
    along_x, along_y, along_z = (direction[0], direction[1], direction[2])
    square = along_x * along_x + along_y * along_y + along_z * along_z
    return jnp.stack([jnp.ones_like(along_x), along_x, along_y, along_z, along_x * along_y, along_y * along_z, along_x * along_z, along_x * along_x - along_y * along_y, 3.0 * along_z * along_z - square])

def atom_energies(own_pos, ghost_pos, center, neigh_all, neighbour_ids, counts, w_radial, w_two, w_env, w_tensor, w_latent, w_out):
    neigh_count = neighbour_ids.shape[0]
    atom_count = own_pos.shape[1]
    blocks = jnp.arange(9)
    shift_x = (blocks // 3 - 1).astype(own_pos.dtype) * box_side
    shift_y = (blocks % 3 - 1).astype(own_pos.dtype) * box_side
    offset = jnp.stack([shift_x, shift_y, jnp.zeros_like(shift_x)], axis=1)
    placed = ghost_pos + offset[:, :, None]
    ghosts = jnp.transpose(placed, (1, 0, 2)).reshape(3, -1)
    every_pos = jnp.concatenate([own_pos, ghosts], axis=1)
    flat_ids = neighbour_ids.reshape(-1)
    far_pos = jnp.take(every_pos, flat_ids, axis=1)
    near_pos = jnp.tile(own_pos, (1, neigh_count))
    offset_vec = far_pos - near_pos
    distance = jnp.sqrt(lax.optimization_barrier(jnp.sum(offset_vec * offset_vec, axis=0)) + core_sq)
    direction = offset_vec / distance[None, :]
    harmonic = harmonics(direction)
    envelope = jnp.exp(-distance * distance / env_width)
    slot_index = jnp.arange(neigh_count)[:, None]
    in_list = (slot_index < counts[None, :]).astype(own_pos.dtype).reshape(-1)
    weight_edge = envelope * in_list
    radial_basis = gaussian_basis(distance, w_radial.shape[0])
    pair_sum = jnp.tile(center, (neigh_count, 1)) + jnp.take(neigh_all, flat_ids, axis=0).astype(center.dtype)
    pair_sum = pair_sum + jnp.dot(radial_basis, w_radial, precision=lax.Precision.HIGHEST)
    first_latent = jax.nn.silu(pair_sum).astype(jnp.bfloat16)
    latent = jax.nn.silu(jnp.dot(first_latent, w_two, preferred_element_type=jnp.float32))
    harmonic_grid = harmonic.reshape(9, neigh_count, atom_count)
    for layer_index in range(w_env.shape[0]):
        latent_bf = latent.astype(jnp.bfloat16)
        env_weight = jnp.dot(latent_bf, w_env[layer_index], preferred_element_type=jnp.float32) * weight_edge[:, None]
        channel = jnp.dot(latent_bf, w_tensor[layer_index], preferred_element_type=jnp.float32)
        env_grid = env_weight.reshape(neigh_count, atom_count, -1)
        summed = 0.25 * jnp.einsum('kac,mka->mca', env_grid, harmonic_grid, precision=lax.Precision.HIGHEST)
        pieces = []
        for start_m, stop_m in ((0, 1), (1, 4), (4, 9)):
            pieces.append(jnp.einsum('mka,mca->kac', harmonic_grid[start_m:stop_m], summed[start_m:stop_m], precision=lax.Precision.HIGHEST))
        grouped = jnp.concatenate(pieces, axis=-1).reshape(neigh_count * atom_count, -1)
        scalars = (grouped * jnp.tile(channel, (1, 3))).astype(jnp.bfloat16)
        joined = jnp.concatenate([latent_bf, scalars], axis=1)
        latent = latent + jax.nn.silu(jnp.dot(joined, w_latent[layer_index], preferred_element_type=jnp.float32))
    out_bf = latent.astype(jnp.bfloat16)
    edge_energy = jnp.dot(out_bf, w_out, preferred_element_type=jnp.float32) * weight_edge
    return lax.optimization_barrier(jnp.sum(edge_energy.reshape(neigh_count, atom_count), axis=0))

def reference(positions, species, charges, neighbours, counts, send_list, species_table, charge_weight, w_center, w_neigh, w_radial, w_two, w_env, w_tensor, w_latent, w_out):
    slabs, columns = (positions.shape[0], positions.shape[1])
    atom_count = positions.shape[3]
    width = w_center.shape[0]
    hidden_all = node_hidden(species.reshape(-1).astype(jnp.float32), charges.reshape(-1), species_table, charge_weight)
    center = jnp.dot(hidden_all, w_center, preferred_element_type=jnp.float32).reshape(slabs, columns, atom_count, width)
    neigh = jnp.dot(hidden_all, w_neigh, preferred_element_type=jnp.float32).astype(jnp.bfloat16)
    neigh = neigh.reshape(slabs, columns, atom_count, width)
    send_pos = jnp.take_along_axis(positions, send_list[:, :, None, :], axis=3)
    send_neigh = jnp.take_along_axis(neigh, send_list[:, :, :, None], axis=2)
    pos_blocks = []
    neigh_blocks = []
    for block_index in range(9):
        step_x = block_index // 3 - 1
        step_y = block_index % 3 - 1
        pos_blocks.append(jnp.roll(send_pos, (-step_x, -step_y), axis=(0, 1)))
        neigh_blocks.append(jnp.roll(send_neigh, (-step_x, -step_y), axis=(0, 1)))
    ghost_pos = jnp.stack(pos_blocks, axis=2)
    ghost_neigh = jnp.stack(neigh_blocks, axis=2).reshape(slabs, columns, -1, width)
    domains = slabs * columns

    def one_domain(items):
        own_pos, ghost_one, center_one, own_neigh, ghost_neigh_one, neighbour_ids, count_one = items
        neigh_all = jnp.concatenate([own_neigh, ghost_neigh_one], axis=0)

        def energy_of(own_value, ghost_value):
            return atom_energies(own_value, ghost_value, center_one, neigh_all, neighbour_ids, count_one, w_radial, w_two, w_env, w_tensor, w_latent, w_out)
        energies, pullback = jax.vjp(energy_of, own_pos, ghost_one)
        grad_own, grad_ghost = pullback(jnp.ones_like(energies))
        return (energies, grad_own, grad_ghost)
    flat_items = (positions.reshape(domains, 3, atom_count), ghost_pos.reshape((domains,) + ghost_pos.shape[2:]), center.reshape(domains, atom_count, width), neigh.reshape(domains, atom_count, width), ghost_neigh.reshape((domains,) + ghost_neigh.shape[2:]), neighbours.reshape((domains,) + neighbours.shape[2:]), counts.reshape(domains, atom_count))
    energies, grad_own, grad_ghost = lax.map(one_domain, flat_items)
    energies = energies.reshape(slabs, columns, atom_count)
    grad_own = grad_own.reshape(slabs, columns, 3, atom_count)
    grad_ghost = grad_ghost.reshape((slabs, columns) + grad_ghost.shape[1:])
    returned = jnp.zeros_like(send_pos)
    for block_index in range(9):
        step_x = block_index // 3 - 1
        step_y = block_index % 3 - 1
        returned = returned + jnp.roll(grad_ghost[:, :, block_index], (step_x, step_y), axis=(0, 1))

    def add_back(own_grad, back_grad, sends):
        return own_grad.at[:, sends].add(back_grad)
    total = jax.vmap(jax.vmap(add_back))(grad_own, returned, send_list)
    return (energies, -total)
```

```python
import jax
import jax.numpy as jnp
from jax import lax
from jax.experimental import pallas as pl
from jax.experimental.pallas import tpu as pltpu
from jax.sharding import PartitionSpec as P

box_side = 3.0
f32 = jnp.float32
bf16 = jnp.bfloat16


def groups_of(shift):
    slabs, columns = lax.axis_size("gx"), lax.axis_size("yz")
    return [
        [
            (2 * m + shift + a) % slabs * columns + (2 * n + shift + b) % columns
            for a in (0, 1)
            for b in (0, 1)
        ]
        for m in range(slabs // 2)
        for n in range(columns // 2)
    ]


def swap(value, shift):
    return lax.all_to_all(value, ("gx", "yz"), 0, 0, axis_index_groups=groups_of(shift))


def halves(value):
    high = lax.reduce_precision(value, 8, 7)
    return high, lax.reduce_precision(value - high, 8, 7)


def thirds(value):
    high, mid = halves(value)
    return high, mid, lax.reduce_precision(value - high - mid, 8, 7)


def mm(a, b):
    return jnp.dot(a, b, preferred_element_type=f32)


def half_turn(x):
    return x + pltpu.roll(x, 64, 1)


def sigmoid(x):
    return 0.5 * jnp.tanh(0.5 * x) + 0.5


def edge_kernel(
    blocks_ref,
    nb_ref,
    count_ref,
    w_kind_ref,
    w_pair_ref,
    w_center_t_ref,
    w_two_t_ref,
    w_ec_t_ref,
    w_lat_t_ref,
    w_two_ref,
    w_back_ref,
    w_scal_ref,
    w_rad_ref,
    w_out_row_ref,
    cols_ref,
    grad_ref,
    energy_ref,
    lat_ref,
    ds1_ref,
    ds2_ref,
    lb_ref,
    er_ref,
    ch_ref,
    s_ref,
    dg_ref,
    du_ref,
    dch_ref,
    dsum_ref,
    rows_ref,
):
    odd_x = lax.rem(lax.axis_index("gx"), 2)
    odd_y = lax.rem(lax.axis_index("yz"), 2)

    def block(b):
        u = 2 - odd_x + (b // 3 - 1)
        v = 2 - odd_y + (b % 3 - 1)
        far = (u // 2) * 2 + v // 2
        near = (u % 2) * 2 + v % 2
        return blocks_ref[far, pl.ds(pl.multiple_of(near * 8, 8), 8), :]

    tables = [block(b) for b in range(9)]

    ids = jnp.concatenate([nb_ref[0:8, :], nb_ref[8:16, :]], axis=1)
    count = jnp.concatenate([count_ref[...], count_ref[...]], axis=1)
    row = lax.broadcasted_iota(jnp.int32, (8, 128), 0)
    lane = lax.broadcasted_iota(jnp.int32, (8, 128), 1)
    slot = row + jnp.where(lane >= 64, 8, 0)
    live = jnp.where(slot < count, 1.0, 0.0)
    own = ids < 64
    beyond = ids - 64
    blk = jnp.zeros_like(ids)
    for b in range(1, 9):
        blk = blk + jnp.where(beyond >= 56 * b, 1, 0)
    place = jnp.where(own, ids, beyond - 56 * blk)
    blk = jnp.where(own, 4, blk)

    def pick(which, index, start):
        out = start
        for b in range(9):
            table = jnp.broadcast_to(tables[b][which : which + 1, :], (8, 128))
            value = jnp.take_along_axis(table, index, axis=1, mode="promise_in_bounds")
            out = jnp.where(blk == b, value, out)
        return out

    listed = pick(5, place, jnp.zeros((8, 128), f32)).astype(jnp.int32)
    atom = jnp.where(own, ids, listed)
    zero = jnp.zeros((8, 128), f32)
    far_x, far_y, far_z, far_q, far_s = [pick(i, atom, zero) for i in range(5)]
    step_x = jnp.where(blk >= 6, 1, jnp.where(blk >= 3, 0, -1))
    step_y = blk - 3 * (step_x + 1) - 1
    mine = tables[4]
    off_x = far_x + box_side * step_x.astype(f32) - mine[0:1, :]
    off_y = far_y + box_side * step_y.astype(f32) - mine[1:2, :]
    off_z = far_z - mine[2:3, :]
    square = off_x * off_x + off_y * off_y + off_z * off_z + 1.0
    dist = jnp.sqrt(square)
    inv = 1.0 / dist
    x, y, z = off_x * inv, off_y * inv, off_z * inv
    harm = [
        None,
        x,
        y,
        z,
        x * y,
        y * z,
        x * z,
        x * x - y * y,
        2.0 * z * z - x * x - y * y,
    ]
    weight = jnp.exp(square * (-1.0 / 32.0)) * live

    kind_row = lax.broadcasted_iota(jnp.int32, (8, 128), 0).astype(f32)
    cw = jnp.broadcast_to(cols_ref[:, 0:1], (128, 128))
    wo = jnp.broadcast_to(cols_ref[:, 1:2], (128, 128))
    cw2 = jnp.concatenate([cw, cw], axis=1)
    wo2 = jnp.concatenate([wo, wo], axis=1)
    centres = 1.0 + lax.broadcasted_iota(jnp.int32, (8, 256), 0).astype(f32)

    def hidden(kind, charge, wide_cw, wide_row):
        onehot = jnp.where(kind == wide_row, 1.0, 0.0)
        pad = jnp.zeros_like(onehot)
        rhs = jnp.concatenate([onehot, onehot, onehot, pad], axis=0).astype(bf16)
        mixed = mm(w_kind_ref[...], rhs) + wide_cw * charge
        return mixed * sigmoid(mixed)

    center = mm(
        w_center_t_ref[...], hidden(mine[4:5, :], mine[3:4, :], cw, kind_row).astype(bf16)
    )
    center2 = jnp.concatenate([center, center], axis=1)
    kind_row2 = jnp.concatenate([kind_row, kind_row], axis=1)

    def wide(packed, c):
        return jnp.concatenate([packed[2 * c : 2 * c + 1, :], packed[2 * c + 1 : 2 * c + 2, :]], axis=1)

    def basis(c):
        spread = wide(dist, c) - centres
        return spread, jnp.exp(-2.0 * spread * spread)

    for c in range(4):
        at = slice(256 * c, 256 * c + 256)
        hid = hidden(wide(far_s, c), wide(far_q, c), cw2, kind_row2)
        _, rb = basis(c)
        rb_high = rb.astype(bf16).astype(f32)
        rhs = jnp.concatenate([hid, rb_high, rb_high, rb - rb_high, jnp.zeros_like(rb)], axis=0)
        pair = mm(w_pair_ref[...], rhs.astype(bf16)) + center2
        sig = sigmoid(pair)
        act = pair * sig
        ds1_ref[:, at] = sig + act * (1.0 - sig)
        second = mm(w_two_t_ref[...], act.astype(bf16))
        sig = sigmoid(second)
        latent = second * sig
        ds2_ref[:, at] = sig + latent * (1.0 - sig)
        lat_ref[:, at] = latent
        latent_bf = latent.astype(bf16)
        lb_ref[:, at] = latent_bf
        both = mm(w_ec_t_ref[...], latent_bf)
        er_ref[:, at] = both[:64]
        ch_ref[:, at] = both[64:]

    def row_of(packed, r):
        return packed[r : r + 1, :]

    def lanes(r):
        return slice(128 * r, 128 * r + 128)

    group_of = [0, 1, 1, 1, 2, 2, 2, 2, 2]
    weighted = [None] + [h * weight for h in harm[1:]]
    for m in range(9):
        scale = weight if m == 0 else weighted[m]
        total = er_ref[:, lanes(0)] * row_of(scale, 0)
        for r in range(1, 8):
            total = total + er_ref[:, lanes(r)] * row_of(scale, r)
        s_ref[m] = 0.25 * half_turn(total)

    def double(value):
        return jnp.concatenate([value, value], axis=1)

    def keep_row(index, c, value):
        rows_ref[index, 2 * c : 2 * c + 1, :] = value[:, :128]
        rows_ref[index, 2 * c + 1 : 2 * c + 2, :] = value[:, 128:]

    for c in range(4):
        at = slice(256 * c, 256 * c + 256)
        channel = ch_ref[:, at]
        grouped = [double(s_ref[0]), None, None]
        for m in range(1, 9):
            term = double(s_ref[m]) * wide(harm[m], c)
            g = group_of[m]
            grouped[g] = term if grouped[g] is None else grouped[g] + term
        scalars = [(g * channel).astype(bf16) for g in grouped]
        joined = jnp.concatenate([lb_ref[:, at]] + scalars, axis=0)
        update = mm(w_lat_t_ref[...], joined)
        sig = sigmoid(update)
        act = update * sig
        out_bf = (lat_ref[:, at] + act).astype(bf16)
        keep_row(0, c, mm(w_out_row_ref[...], out_bf)[0:1])
        d_update = (wo2 * wide(weight, c) * (sig + act * (1.0 - sig))).astype(bf16)
        du_ref[:, at] = d_update
        d_scal = mm(w_scal_ref[...], d_update)
        d_grouped = []
        d_channel = None
        for g in range(3):
            part = d_scal[64 * g : 64 * g + 64]
            term = part * grouped[g]
            d_channel = term if d_channel is None else d_channel + term
            d_grouped.append(part * channel)
            dg_ref[g, :, at] = d_grouped[g]
        dch_ref[:, at] = d_channel.astype(bf16)
        for m in range(1, 9):
            keep_row(m, c, jnp.sum(d_grouped[group_of[m]] * double(s_ref[m]), axis=0, keepdims=True))

    for m in range(9):
        g = group_of[m]
        total = None
        for r in range(8):
            term = dg_ref[g, :, lanes(r)]
            if m > 0:
                term = term * row_of(harm[m], r)
            total = term if total is None else total + term
        dsum_ref[m] = 0.25 * half_turn(total)

    for c in range(4):
        at = slice(256 * c, 256 * c + 256)
        raw = er_ref[:, at]
        w_row = wide(weight, c)
        d_env = double(dsum_ref[0])
        for m in range(1, 9):
            back = double(dsum_ref[m])
            d_env = d_env + back * wide(harm[m], c)
            keep_row(8 + m, c, jnp.sum(raw * back, axis=0, keepdims=True))
        keep_row(17, c, jnp.sum(raw * d_env, axis=0, keepdims=True))
        d_joined = jnp.concatenate(
            [du_ref[:, at], (d_env * w_row).astype(bf16), dch_ref[:, at]], axis=0
        )
        d_latent = mm(w_back_ref[...], d_joined) + wo2 * w_row
        d_second = (d_latent * ds2_ref[:, at]).astype(bf16)
        d_pair = mm(w_two_ref[...], d_second) * ds1_ref[:, at]
        high = d_pair.astype(bf16)
        low = (d_pair - high.astype(f32)).astype(bf16)
        first = mm(w_rad_ref[...], high)
        d_basis = first[0:8] + first[8:16] + mm(w_rad_ref[...], low)[0:8]
        spread, rb = basis(c)
        keep_row(18, c, jnp.sum(d_basis * rb * spread, axis=0, keepdims=True) * -4.0)

    energy = jnp.sum(rows_ref[0] * weight, axis=0, keepdims=True)
    energy_ref[...] = half_turn(energy)[:, :64]
    d_h = [None] + [rows_ref[m] + weight * rows_ref[8 + m] for m in range(1, 9)]
    g_x = d_h[1] + y * d_h[4] + z * d_h[6] + 2.0 * x * (d_h[7] - d_h[8])
    g_y = d_h[2] + x * d_h[4] + z * d_h[5] - 2.0 * y * (d_h[7] + d_h[8])
    g_z = d_h[3] + y * d_h[5] + x * d_h[6] + 4.0 * z * d_h[8]
    d_weight = rows_ref[0] + rows_ref[17]
    d_dist = (
        rows_ref[18]
        - inv * (g_x * x + g_y * y + g_z * z)
        - d_weight * weight * dist * (1.0 / 16.0)
    )
    e_x = g_x * inv + d_dist * x
    e_y = g_y * inv + d_dist * y
    e_z = g_z * inv + d_dist * z

    u = 1 + odd_x + step_x
    v = 1 + odd_y + step_y
    target = ((u // 2) * 2 + v // 2) * 4 + (u % 2) * 2 + v % 2
    atom_row = lax.broadcasted_iota(jnp.int32, (64, 128), 0)
    pairs_row = lax.broadcasted_iota(jnp.int32, (8, 128), 0)
    part_row = lax.rem(pairs_row, 4)
    left, right = [], []
    for r in range(8):
        mixed = jnp.where(
            part_row == 0,
            row_of(e_x, r),
            jnp.where(part_row == 1, row_of(e_y, r), jnp.where(part_row == 2, row_of(e_z, r), 0.0)),
        )
        high = mixed.astype(bf16).astype(f32)
        low = mixed - high
        goal = jnp.broadcast_to(row_of(target, r), (8, 128)) - jnp.where(pairs_row >= 4, 1, 0)
        stack = [jnp.where(goal == 2 * i, high, 0.0) for i in range(8)]
        stack += [jnp.where(goal == 2 * i, low, 0.0) for i in range(8)]
        left.append(jnp.concatenate(stack, axis=0).astype(bf16))
        right.append(jnp.where(atom_row == row_of(atom, r), 1.0, 0.0).astype(bf16))
    far = lax.dot_general(
        jnp.concatenate(left, axis=1),
        jnp.concatenate(right, axis=1),
        (((1,), (1,)), ((), ())),
        preferred_element_type=f32,
    )
    far = far[:64] + far[64:]
    near = jnp.concatenate(
        [half_turn(jnp.sum(e, axis=0, keepdims=True))[:, :64] for e in (e_x, e_y, e_z)]
        + [jnp.zeros((1, 64), f32)],
        axis=0,
    )
    near = jnp.concatenate([near, near], axis=0)
    home = ((1 + odd_x) // 2 * 2 + (1 + odd_y) // 2) * 4 + lax.rem(1 + odd_x, 2) * 2 + lax.rem(1 + odd_y, 2)
    half_row = jnp.where(lax.broadcasted_iota(jnp.int32, (8, 64), 0) >= 4, 1, 0)
    for i in range(8):
        here = far[8 * i : 8 * i + 8]
        grad_ref[i // 2, 8 * (i % 2) : 8 * (i % 2) + 8, :] = here - jnp.where(
            half_row + 2 * i == home, near, 0.0
        )


def local(
    positions,
    species,
    charges,
    neighbours,
    counts,
    send_list,
    species_table,
    charge_weight,
    w_center,
    w_neigh,
    w_radial,
    w_two,
    w_env,
    w_tensor,
    w_latent,
    w_out,
):
    sends = jnp.pad(send_list[0].astype(f32), ((0, 0), (0, 8)))
    mine = jnp.concatenate(
        [positions[0, 0], charges[0], species[0].astype(f32), sends, jnp.zeros((2, 64), f32)],
        axis=0,
    )
    mine = jnp.concatenate([mine, mine], axis=1)
    four = swap(jnp.broadcast_to(mine[None], (4, 8, 128)), 0).reshape(32, 128)
    blocks = swap(jnp.broadcast_to(four[None], (4, 32, 128)), 1)

    kinds = jnp.pad(species_table, ((0, 2), (0, 0)))
    w_kind = jnp.concatenate([*thirds(kinds), jnp.zeros((8, 128), f32)], axis=0).T.astype(bf16)
    rad_high, rad_low = halves(w_radial)
    w_pair = jnp.concatenate(
        [w_neigh.astype(f32), rad_high, rad_low, rad_high, jnp.zeros((8, 128), f32)], axis=0
    ).T.astype(bf16)
    w_rad = jnp.concatenate([rad_high, rad_low], axis=0).astype(bf16)
    w_ec = jnp.concatenate([w_env[0], w_tensor[0]], axis=1)
    w_back = jnp.concatenate([w_latent[0, :128], w_ec], axis=1)
    w_out_row = jnp.pad(w_out[None], ((0, 15), (0, 0)))
    cols = jnp.stack([charge_weight, w_out.astype(f32)], axis=1)
    operands = (
        blocks,
        neighbours[0, 0],
        counts[0],
        w_kind,
        w_pair,
        w_center.T,
        w_two.T,
        w_ec.T,
        w_latent[0].T,
        w_two,
        w_back,
        w_latent[0, 128:],
        w_rad,
        w_out_row,
        cols,
    )
    vmem = pl.BlockSpec(memory_space=pltpu.VMEM)
    grads, energy = pl.pallas_call(
        edge_kernel,
        out_shape=(
            jax.ShapeDtypeStruct((4, 16, 64), f32),
            jax.ShapeDtypeStruct((1, 64), f32),
        ),
        in_specs=[vmem] * len(operands),
        out_specs=(vmem, vmem),
        scratch_shapes=[
            pltpu.VMEM((128, 1024), f32),
            pltpu.VMEM((128, 1024), f32),
            pltpu.VMEM((128, 1024), f32),
            pltpu.VMEM((128, 1024), bf16),
            pltpu.VMEM((64, 1024), f32),
            pltpu.VMEM((64, 1024), f32),
            pltpu.VMEM((9, 64, 128), f32),
            pltpu.VMEM((3, 64, 1024), f32),
            pltpu.VMEM((128, 1024), bf16),
            pltpu.VMEM((64, 1024), bf16),
            pltpu.VMEM((9, 64, 128), f32),
            pltpu.VMEM((19, 8, 128), f32),
        ],
        compiler_params=pltpu.CompilerParams(vmem_limit_bytes=24 * 1024 * 1024),
        name="edges",
    )(*operands)
    back = jnp.sum(swap(grads, 0), axis=0).reshape(4, 4, 64)
    total = jnp.sum(swap(back, 1), axis=0)
    return (energy[None], -total[None, None, :3])


def solution(mesh):
    return jax.shard_map(
        local,
        mesh=mesh,
        in_specs=(
            P("gx", "yz", None, None),
            P("gx", "yz", None),
            P("gx", "yz", None),
            P("gx", "yz", None, None),
            P("gx", "yz", None),
            P("gx", "yz", None),
            P(),
            P(),
            P(),
            P(),
            P(),
            P(),
            P(),
            P(),
            P(),
            P(),
        ),
        out_specs=(P("gx", "yz", None), P("gx", "yz", None, None)),
        check_vma=False,
    )
```

```python
import jax
import jax.numpy as jnp
from jax import lax
from jax.experimental import pallas as pl
from jax.experimental.pallas import tpu as pltpu
from jax.sharding import PartitionSpec as P

box_side = 3.0
f32 = jnp.float32
bf16 = jnp.bfloat16


def groups_of(shift):
    slabs, columns = lax.axis_size("gx"), lax.axis_size("yz")
    return [
        [
            (2 * m + shift + a) % slabs * columns + (2 * n + shift + b) % columns
            for a in (0, 1)
            for b in (0, 1)
        ]
        for m in range(slabs // 2)
        for n in range(columns // 2)
    ]


def swap(value, shift):
    return lax.all_to_all(value, ("gx", "yz"), 0, 0, axis_index_groups=groups_of(shift))


def halves(value):
    high = value.astype(bf16).astype(f32)
    return high, value - high


def turned(value):
    return value.astype(f32).T.astype(bf16)


def mm(a, b):
    return jnp.dot(a, b, preferred_element_type=f32)


def half_turn(x):
    return x + pltpu.roll(x, 64, 1)


def sigmoid(x):
    return 0.5 * jnp.tanh(0.5 * x) + 0.5


def pack_kernel(pos_ref, charge_ref, kind_ref, send_ref, out_ref):
    out_ref[...] = jnp.zeros_like(out_ref)
    for k in range(4):
        for i in range(3):
            out_ref[k, i : i + 1, 0:64] = pos_ref[i]
        out_ref[k, 3:4, 0:64] = charge_ref[...]
        out_ref[k, 4:5, 0:64] = kind_ref[...].astype(f32)
        out_ref[k, 5:6, 0:56] = send_ref[...].astype(f32)


def force_kernel(parts_ref, out_ref):
    total = parts_ref[0] + parts_ref[1] + parts_ref[2] + parts_ref[3]
    for i in range(3):
        out_ref[i] = -total[i : i + 1, 0:64]


def edge_kernel(
    blocks_ref,
    nb_ref,
    count_ref,
    kinds_ref,
    charge_weight_ref,
    w_center_ref,
    w_neigh_ref,
    w_radial_ref,
    w_two_ref,
    w_env_t_ref,
    w_tensor_t_ref,
    w_latent_ref,
    w_out_ref,
    grad_ref,
    energy_ref,
    lat_ref,
    ds1_ref,
    ds2_ref,
    lb_ref,
    er_ref,
    ch_ref,
    s_ref,
    dg_ref,
    du_ref,
    dch_ref,
    dsum_ref,
    rows_ref,
    kinds8_ref,
):
    kinds8_ref[...] = jnp.zeros_like(kinds8_ref)
    kinds8_ref[0:6, :] = kinds_ref[...]
    kind_high, rest = halves(kinds8_ref[...])
    kind_mid, kind_low = halves(rest)
    rad_high, rad_low = halves(w_radial_ref[...])
    none = jnp.zeros((8, 128), f32)
    small = jnp.concatenate(
        [rad_high, rad_low, rad_high, none, kind_high, kind_mid, kind_low, none, jnp.zeros((64, 128), f32)],
        axis=0,
    ).T.astype(bf16)
    w_pair = jnp.concatenate([turned(w_neigh_ref[...]), small[:, 0:32]], axis=1)
    w_kind = small[:, 32:64]
    w_rad = jnp.concatenate([rad_high, rad_low], axis=0).astype(bf16)
    w_center_t = turned(w_center_ref[...])
    w_two_t = turned(w_two_ref[...])
    w_lat_t = jnp.concatenate(
        [turned(w_latent_ref[0:128, :]), turned(w_latent_ref[128:256, :]), turned(w_latent_ref[256:320, :])],
        axis=1,
    )
    w_ec_t = jnp.concatenate([w_env_t_ref[...], w_tensor_t_ref[...]], axis=0)
    w_back = jnp.concatenate([w_latent_ref[0:128, :], turned(w_ec_t)], axis=1)
    w_scal = w_latent_ref[128:320, :]
    w_out = w_out_ref[...].astype(f32)
    w_out_row = jnp.broadcast_to(w_out, (16, 128)).astype(bf16)
    cw = jnp.broadcast_to(charge_weight_ref[...], (128, 128)).T
    wo = jnp.broadcast_to(w_out, (128, 128)).T

    odd_x = lax.rem(lax.axis_index("gx"), 2)
    odd_y = lax.rem(lax.axis_index("yz"), 2)

    def block(b):
        u = 2 - odd_x + (b // 3 - 1)
        v = 2 - odd_y + (b % 3 - 1)
        far = (u // 2) * 2 + v // 2
        near = (u % 2) * 2 + v % 2
        return blocks_ref[far, pl.ds(pl.multiple_of(near * 8, 8), 8), :]

    tables = [block(b) for b in range(9)]

    ids = jnp.concatenate([nb_ref[0:8, :], nb_ref[8:16, :]], axis=1)
    count = jnp.concatenate([count_ref[...], count_ref[...]], axis=1)
    row = lax.broadcasted_iota(jnp.int32, (8, 128), 0)
    lane = lax.broadcasted_iota(jnp.int32, (8, 128), 1)
    slot = row + jnp.where(lane >= 64, 8, 0)
    live = jnp.where(slot < count, 1.0, 0.0)
    own = ids < 64
    beyond = ids - 64
    blk = jnp.zeros_like(ids)
    for b in range(1, 9):
        blk = blk + jnp.where(beyond >= 56 * b, 1, 0)
    place = jnp.where(own, ids, beyond - 56 * blk)
    blk = jnp.where(own, 4, blk)

    def pick(which, index, start):
        out = start
        for b in range(9):
            table = jnp.broadcast_to(tables[b][which : which + 1, :], (8, 128))
            value = jnp.take_along_axis(table, index, axis=1, mode="promise_in_bounds")
            out = jnp.where(blk == b, value, out)
        return out

    listed = pick(5, place, jnp.zeros((8, 128), f32)).astype(jnp.int32)
    atom = jnp.where(own, ids, listed)
    zero = jnp.zeros((8, 128), f32)
    far_x, far_y, far_z, far_q, far_s = [pick(i, atom, zero) for i in range(5)]
    step_x = jnp.where(blk >= 6, 1, jnp.where(blk >= 3, 0, -1))
    step_y = blk - 3 * (step_x + 1) - 1
    mine = half_turn(tables[4])
    off_x = far_x + box_side * step_x.astype(f32) - mine[0:1, :]
    off_y = far_y + box_side * step_y.astype(f32) - mine[1:2, :]
    off_z = far_z - mine[2:3, :]
    square = off_x * off_x + off_y * off_y + off_z * off_z + 1.0
    dist = jnp.sqrt(square)
    inv = 1.0 / dist
    x, y, z = off_x * inv, off_y * inv, off_z * inv
    harm = [
        None,
        x,
        y,
        z,
        x * y,
        y * z,
        x * z,
        x * x - y * y,
        2.0 * z * z - x * x - y * y,
    ]
    weight = jnp.exp(square * (-1.0 / 32.0)) * live

    kind_row = lax.broadcasted_iota(jnp.int32, (8, 128), 0).astype(f32)
    cw2 = jnp.concatenate([cw, cw], axis=1)
    wo2 = jnp.concatenate([wo, wo], axis=1)
    centres = 1.0 + lax.broadcasted_iota(jnp.int32, (8, 256), 0).astype(f32)

    def hidden(kind, charge, wide_cw, wide_row):
        onehot = jnp.where(kind == wide_row, 1.0, 0.0)
        pad = jnp.zeros_like(onehot)
        rhs = jnp.concatenate([onehot, onehot, onehot, pad], axis=0).astype(bf16)
        mixed = mm(w_kind, rhs) + wide_cw * charge
        return mixed * sigmoid(mixed)

    center = mm(
        w_center_t, hidden(mine[4:5, :], mine[3:4, :], cw, kind_row).astype(bf16)
    )
    center2 = jnp.concatenate([center, center], axis=1)
    kind_row2 = jnp.concatenate([kind_row, kind_row], axis=1)

    def wide(packed, c):
        return jnp.concatenate([packed[2 * c : 2 * c + 1, :], packed[2 * c + 1 : 2 * c + 2, :]], axis=1)

    def basis(c):
        spread = wide(dist, c) - centres
        return spread, jnp.exp(-2.0 * spread * spread)

    for c in range(4):
        at = slice(256 * c, 256 * c + 256)
        hid = hidden(wide(far_s, c), wide(far_q, c), cw2, kind_row2)
        _, rb = basis(c)
        rb_high = rb.astype(bf16).astype(f32)
        rhs = jnp.concatenate([hid, rb_high, rb_high, rb - rb_high, jnp.zeros_like(rb)], axis=0)
        pair = mm(w_pair, rhs.astype(bf16)) + center2
        sig = sigmoid(pair)
        act = pair * sig
        ds1_ref[:, at] = sig + act * (1.0 - sig)
        second = mm(w_two_t, act.astype(bf16))
        sig = sigmoid(second)
        latent = second * sig
        ds2_ref[:, at] = sig + latent * (1.0 - sig)
        lat_ref[:, at] = latent
        latent_bf = latent.astype(bf16)
        lb_ref[:, at] = latent_bf
        both = mm(w_ec_t, latent_bf)
        er_ref[:, at] = both[:64]
        ch_ref[:, at] = both[64:]

    def row_of(packed, r):
        return packed[r : r + 1, :]

    def lanes(r):
        return slice(128 * r, 128 * r + 128)

    group_of = [0, 1, 1, 1, 2, 2, 2, 2, 2]
    weighted = [None] + [h * weight for h in harm[1:]]
    for m in range(9):
        scale = weight if m == 0 else weighted[m]
        total = er_ref[:, lanes(0)] * row_of(scale, 0)
        for r in range(1, 8):
            total = total + er_ref[:, lanes(r)] * row_of(scale, r)
        s_ref[m] = 0.25 * half_turn(total)

    def double(value):
        return jnp.concatenate([value, value], axis=1)

    def keep_row(index, c, value):
        rows_ref[index, 2 * c : 2 * c + 1, :] = value[:, :128]
        rows_ref[index, 2 * c + 1 : 2 * c + 2, :] = value[:, 128:]

    for c in range(4):
        at = slice(256 * c, 256 * c + 256)
        channel = ch_ref[:, at]
        grouped = [double(s_ref[0]), None, None]
        for m in range(1, 9):
            term = double(s_ref[m]) * wide(harm[m], c)
            g = group_of[m]
            grouped[g] = term if grouped[g] is None else grouped[g] + term
        scalars = [(g * channel).astype(bf16) for g in grouped]
        joined = jnp.concatenate([lb_ref[:, at]] + scalars, axis=0)
        update = mm(w_lat_t, joined)
        sig = sigmoid(update)
        act = update * sig
        out_bf = (lat_ref[:, at] + act).astype(bf16)
        keep_row(0, c, mm(w_out_row, out_bf)[0:1])
        d_update = (wo2 * wide(weight, c) * (sig + act * (1.0 - sig))).astype(bf16)
        du_ref[:, at] = d_update
        d_scal = mm(w_scal, d_update)
        d_grouped = []
        d_channel = None
        for g in range(3):
            part = d_scal[64 * g : 64 * g + 64]
            term = part * grouped[g]
            d_channel = term if d_channel is None else d_channel + term
            d_grouped.append(part * channel)
            dg_ref[g, :, at] = d_grouped[g]
        dch_ref[:, at] = d_channel.astype(bf16)
        for m in range(1, 9):
            keep_row(m, c, jnp.sum(d_grouped[group_of[m]] * double(s_ref[m]), axis=0, keepdims=True))

    for m in range(9):
        g = group_of[m]
        total = None
        for r in range(8):
            term = dg_ref[g, :, lanes(r)]
            if m > 0:
                term = term * row_of(harm[m], r)
            total = term if total is None else total + term
        dsum_ref[m] = 0.25 * half_turn(total)

    for c in range(4):
        at = slice(256 * c, 256 * c + 256)
        raw = er_ref[:, at]
        w_row = wide(weight, c)
        d_env = double(dsum_ref[0])
        for m in range(1, 9):
            back = double(dsum_ref[m])
            d_env = d_env + back * wide(harm[m], c)
            keep_row(8 + m, c, jnp.sum(raw * back, axis=0, keepdims=True))
        keep_row(17, c, jnp.sum(raw * d_env, axis=0, keepdims=True))
        d_joined = jnp.concatenate(
            [du_ref[:, at], (d_env * w_row).astype(bf16), dch_ref[:, at]], axis=0
        )
        d_latent = mm(w_back, d_joined) + wo2 * w_row
        d_second = (d_latent * ds2_ref[:, at]).astype(bf16)
        d_pair = mm(w_two_ref[...], d_second) * ds1_ref[:, at]
        high = d_pair.astype(bf16)
        low = (d_pair - high.astype(f32)).astype(bf16)
        first = mm(w_rad, high)
        d_basis = first[0:8] + first[8:16] + mm(w_rad, low)[0:8]
        spread, rb = basis(c)
        keep_row(18, c, jnp.sum(d_basis * rb * spread, axis=0, keepdims=True) * -4.0)

    energy = jnp.sum(rows_ref[0] * weight, axis=0, keepdims=True)
    energy_ref[...] = half_turn(energy)[:, :64]
    d_h = [None] + [rows_ref[m] + weight * rows_ref[8 + m] for m in range(1, 9)]
    g_x = d_h[1] + y * d_h[4] + z * d_h[6] + 2.0 * x * (d_h[7] - d_h[8])
    g_y = d_h[2] + x * d_h[4] + z * d_h[5] - 2.0 * y * (d_h[7] + d_h[8])
    g_z = d_h[3] + y * d_h[5] + x * d_h[6] + 4.0 * z * d_h[8]
    d_weight = rows_ref[0] + rows_ref[17]
    d_dist = (
        rows_ref[18]
        - inv * (g_x * x + g_y * y + g_z * z)
        - d_weight * weight * dist * (1.0 / 16.0)
    )
    e_x = g_x * inv + d_dist * x
    e_y = g_y * inv + d_dist * y
    e_z = g_z * inv + d_dist * z

    u = 1 + odd_x + step_x
    v = 1 + odd_y + step_y
    target = ((u // 2) * 2 + v // 2) * 4 + (u % 2) * 2 + v % 2
    atom_row = lax.broadcasted_iota(jnp.int32, (64, 128), 0)
    pairs_row = lax.broadcasted_iota(jnp.int32, (8, 128), 0)
    part_row = lax.rem(pairs_row, 4)
    left, right = [], []
    for r in range(8):
        mixed = jnp.where(
            part_row == 0,
            row_of(e_x, r),
            jnp.where(part_row == 1, row_of(e_y, r), jnp.where(part_row == 2, row_of(e_z, r), 0.0)),
        )
        high = mixed.astype(bf16).astype(f32)
        low = mixed - high
        goal = jnp.broadcast_to(row_of(target, r), (8, 128)) - jnp.where(pairs_row >= 4, 1, 0)
        stack = [jnp.where(goal == 2 * i, high, 0.0) for i in range(8)]
        stack += [jnp.where(goal == 2 * i, low, 0.0) for i in range(8)]
        left.append(jnp.concatenate(stack, axis=0).astype(bf16))
        right.append(jnp.where(atom_row == row_of(atom, r), 1.0, 0.0).astype(bf16))
    far = lax.dot_general(
        jnp.concatenate(left, axis=1),
        jnp.concatenate(right, axis=1),
        (((1,), (1,)), ((), ())),
        preferred_element_type=f32,
    )
    far = far[:64] + far[64:]
    near = jnp.concatenate(
        [half_turn(jnp.sum(e, axis=0, keepdims=True))[:, :64] for e in (e_x, e_y, e_z)]
        + [jnp.zeros((1, 64), f32)],
        axis=0,
    )
    home = ((1 + odd_x) // 2 * 2 + (1 + odd_y) // 2) * 4 + lax.rem(1 + odd_x, 2) * 2 + lax.rem(1 + odd_y, 2)
    grad_ref[...] = jnp.zeros_like(grad_ref)
    for i in range(16):
        here = far[4 * i : 4 * i + 4] - jnp.where(home == i, near, 0.0)
        grad_ref[i // 4, 8 * (i % 4) : 8 * (i % 4) + 4, 0:64] = here


def local(
    positions,
    species,
    charges,
    neighbours,
    counts,
    send_list,
    species_table,
    charge_weight,
    w_center,
    w_neigh,
    w_radial,
    w_two,
    w_env,
    w_tensor,
    w_latent,
    w_out,
):
    vmem = pl.BlockSpec(memory_space=pltpu.VMEM)
    first = pl.pallas_call(
        pack_kernel,
        out_shape=jax.ShapeDtypeStruct((4, 8, 128), f32),
        in_specs=[vmem] * 4,
        out_specs=vmem,
        name="pack",
    )(positions.reshape(3, 1, 64), charges[0], species[0], send_list[0])
    four = swap(first, 0).reshape(32, 128)
    blocks = swap(jnp.broadcast_to(four[None], (4, 32, 128)), 1)
    operands = (
        blocks,
        neighbours[0, 0],
        counts[0],
        species_table,
        charge_weight[None],
        w_center,
        w_neigh,
        w_radial,
        w_two,
        w_env[0].T,
        w_tensor[0].T,
        w_latent[0],
        w_out[None],
    )
    grads, energy = pl.pallas_call(
        edge_kernel,
        out_shape=(
            jax.ShapeDtypeStruct((4, 32, 128), f32),
            jax.ShapeDtypeStruct((1, 64), f32),
        ),
        in_specs=[vmem] * len(operands),
        out_specs=(vmem, vmem),
        scratch_shapes=[
            pltpu.VMEM((128, 1024), f32),
            pltpu.VMEM((128, 1024), f32),
            pltpu.VMEM((128, 1024), f32),
            pltpu.VMEM((128, 1024), bf16),
            pltpu.VMEM((64, 1024), f32),
            pltpu.VMEM((64, 1024), f32),
            pltpu.VMEM((9, 64, 128), f32),
            pltpu.VMEM((3, 64, 1024), f32),
            pltpu.VMEM((128, 1024), bf16),
            pltpu.VMEM((64, 1024), bf16),
            pltpu.VMEM((9, 64, 128), f32),
            pltpu.VMEM((19, 8, 128), f32),
            pltpu.VMEM((8, 128), f32),
        ],
        compiler_params=pltpu.CompilerParams(vmem_limit_bytes=16 * 1024 * 1024),
        name="edges",
    )(*operands)
    back = jnp.sum(swap(grads, 0), axis=0).reshape(4, 8, 128)
    forces = pl.pallas_call(
        force_kernel,
        out_shape=jax.ShapeDtypeStruct((3, 1, 64), f32),
        in_specs=[vmem],
        out_specs=vmem,
        name="forces",
    )(swap(back, 1))
    return (energy[None], forces.reshape(1, 1, 3, 64))


def solution(mesh):
    return jax.shard_map(
        local,
        mesh=mesh,
        in_specs=(
            P("gx", "yz", None, None),
            P("gx", "yz", None),
            P("gx", "yz", None),
            P("gx", "yz", None, None),
            P("gx", "yz", None),
            P("gx", "yz", None),
            P(),
            P(),
            P(),
            P(),
            P(),
            P(),
            P(),
            P(),
            P(),
            P(),
        ),
        out_specs=(P("gx", "yz", None), P("gx", "yz", None, None)),
        check_vma=False,
    )
```

```python
import jax
import jax.numpy as jnp
from jax import lax
from jax.experimental import pallas as pl
from jax.experimental.pallas import tpu as pltpu
from jax.sharding import PartitionSpec as P

box_side = 3.0
f32 = jnp.float32
bf16 = jnp.bfloat16


FORTH = ((0, 0), (1, 1))
BACK = ((0, 0), (1, 1))


def groups_of(pairing):
    slabs, columns = lax.axis_size("gx"), lax.axis_size("yz")
    return [
        [
            (2 * m + pairing[0] + a) % slabs * columns + (2 * n + pairing[1] + b) % columns
            for a in (0, 1)
            for b in (0, 1)
        ]
        for m in range(slabs // 2)
        for n in range(columns // 2)
    ]


def swap(value, pairing):
    return lax.all_to_all(value, ("gx", "yz"), 0, 0, axis_index_groups=groups_of(pairing))


def centre_of(odd, outer):
    return 2 - odd if outer else 1 + odd


def halves(value):
    high = value.astype(bf16).astype(f32)
    return high, value - high


def turned(value):
    return value.astype(f32).T.astype(bf16)


def mm(a, b):
    return jnp.dot(a, b, preferred_element_type=f32)


def half_turn(x):
    return x + pltpu.roll(x, 64, 1)


def sigmoid(x):
    return 0.5 * jnp.tanh(0.5 * x) + 0.5


def pack_kernel(
    pos_ref,
    charge_ref,
    kind_ref,
    send_ref,
    nb_ref,
    count_ref,
    table_ref,
    charge_weight_ref,
    w_radial_ref,
    w_out_ref,
    out_ref,
    whole_ref,
    small_ref,
):
    out_ref[...] = jnp.zeros_like(out_ref)
    for k in range(4):
        for i in range(3):
            out_ref[k, i : i + 1, 0:64] = pos_ref[i]
        out_ref[k, 3:4, 0:64] = charge_ref[...]
        out_ref[k, 4:5, 0:64] = kind_ref[...].astype(f32)
        out_ref[k, 5:6, 0:56] = send_ref[...].astype(f32)
    whole_ref[0:16, :] = nb_ref[...]
    whole_ref[16:17, :] = count_ref[...]
    small_ref[0:8, :] = jnp.zeros((8, 128), f32)
    small_ref[0:6, :] = table_ref[...]
    small_ref[8:16, :] = w_radial_ref[...]
    small_ref[16:17, :] = charge_weight_ref[...]
    small_ref[17:18, :] = w_out_ref[...].astype(f32)


def force_kernel(parts_ref, out_ref):
    total = parts_ref[0] + parts_ref[1] + parts_ref[2] + parts_ref[3]
    for i in range(3):
        out_ref[i] = -total[i : i + 1, 0:64]


def edge_kernel(
    blocks_ref,
    whole_ref,
    small_ref,
    w_center_ref,
    w_neigh_ref,
    w_two_ref,
    w_env_t_ref,
    w_tensor_t_ref,
    w_latent_ref,
    grad_ref,
    energy_ref,
    lat_ref,
    ds1_ref,
    ds2_ref,
    lb_ref,
    er_ref,
    ch_ref,
    s_ref,
    dg_ref,
    du_ref,
    dch_ref,
    dsum_ref,
    rows_ref,
):
    w_center_t = turned(w_center_ref[...])
    w_neigh_t = turned(w_neigh_ref[...])
    w_two_t = turned(w_two_ref[...])
    w_lat_t = jnp.concatenate(
        [turned(w_latent_ref[0:128, :]), turned(w_latent_ref[128:256, :]), turned(w_latent_ref[256:320, :])],
        axis=1,
    )
    w_ec_t = jnp.concatenate([w_env_t_ref[...], w_tensor_t_ref[...]], axis=0)
    w_back = jnp.concatenate([w_latent_ref[0:128, :], turned(w_ec_t)], axis=1)
    w_scal = w_latent_ref[128:320, :]
    w_out = small_ref[17:18, :]
    w_out_row = jnp.broadcast_to(w_out, (16, 128)).astype(bf16)
    wo = jnp.broadcast_to(w_out, (128, 128)).T
    kind_high, rest = halves(small_ref[0:8, :])
    kind_mid, kind_low = halves(rest)
    rad_high, rad_low = halves(small_ref[8:16, :])
    none = jnp.zeros((8, 128), f32)
    small = jnp.concatenate(
        [rad_high, rad_low, rad_high, none, kind_high, kind_mid, kind_low, none, jnp.zeros((64, 128), f32)],
        axis=0,
    ).T.astype(bf16)
    w_pair = jnp.concatenate([w_neigh_t, small[:, 0:32]], axis=1)
    w_kind = small[:, 32:64]
    w_rad = jnp.concatenate([rad_high, rad_low], axis=0).astype(bf16)
    cw = jnp.broadcast_to(small_ref[16:17, :], (128, 128)).T

    odd_x = lax.rem(lax.axis_index("gx"), 2)
    odd_y = lax.rem(lax.axis_index("yz"), 2)

    def block(b):
        u = centre_of(odd_x, FORTH[1][0]) + (b // 3 - 1)
        v = centre_of(odd_y, FORTH[1][1]) + (b % 3 - 1)
        far = (u // 2) * 2 + v // 2
        near = (u % 2) * 2 + v % 2
        return blocks_ref[far, pl.ds(pl.multiple_of(near * 8, 8), 8), :]

    tables = [block(b) for b in range(9)]

    ids = jnp.concatenate([whole_ref[0:8, :], whole_ref[8:16, :]], axis=1)
    count = jnp.concatenate([whole_ref[16:17, :], whole_ref[16:17, :]], axis=1)
    row = lax.broadcasted_iota(jnp.int32, (8, 128), 0)
    lane = lax.broadcasted_iota(jnp.int32, (8, 128), 1)
    slot = row + jnp.where(lane >= 64, 8, 0)
    live = jnp.where(slot < count, 1.0, 0.0)
    own = ids < 64
    beyond = ids - 64
    blk = jnp.zeros_like(ids)
    for b in range(1, 9):
        blk = blk + jnp.where(beyond >= 56 * b, 1, 0)
    place = jnp.where(own, ids, beyond - 56 * blk)
    blk = jnp.where(own, 4, blk)

    def pick(which, index, start):
        out = start
        for b in range(9):
            table = jnp.broadcast_to(tables[b][which : which + 1, :], (8, 128))
            value = jnp.take_along_axis(table, index, axis=1, mode="promise_in_bounds")
            out = jnp.where(blk == b, value, out)
        return out

    listed = pick(5, place, jnp.zeros((8, 128), f32)).astype(jnp.int32)
    atom = jnp.where(own, ids, listed)
    zero = jnp.zeros((8, 128), f32)
    far_x, far_y, far_z, far_q, far_s = [pick(i, atom, zero) for i in range(5)]
    step_x = jnp.where(blk >= 6, 1, jnp.where(blk >= 3, 0, -1))
    step_y = blk - 3 * (step_x + 1) - 1
    mine = half_turn(tables[4])
    off_x = far_x + box_side * step_x.astype(f32) - mine[0:1, :]
    off_y = far_y + box_side * step_y.astype(f32) - mine[1:2, :]
    off_z = far_z - mine[2:3, :]
    square = off_x * off_x + off_y * off_y + off_z * off_z + 1.0
    dist = jnp.sqrt(square)
    inv = 1.0 / dist
    x, y, z = off_x * inv, off_y * inv, off_z * inv
    harm = [
        None,
        x,
        y,
        z,
        x * y,
        y * z,
        x * z,
        x * x - y * y,
        2.0 * z * z - x * x - y * y,
    ]
    weight = jnp.exp(square * (-1.0 / 32.0)) * live

    kind_row = lax.broadcasted_iota(jnp.int32, (8, 128), 0).astype(f32)
    cw2 = jnp.concatenate([cw, cw], axis=1)
    wo2 = jnp.concatenate([wo, wo], axis=1)
    centres = 1.0 + lax.broadcasted_iota(jnp.int32, (8, 256), 0).astype(f32)

    def hidden(kind, charge, wide_cw, wide_row):
        onehot = jnp.where(kind == wide_row, 1.0, 0.0)
        pad = jnp.zeros_like(onehot)
        rhs = jnp.concatenate([onehot, onehot, onehot, pad], axis=0).astype(bf16)
        mixed = mm(w_kind, rhs) + wide_cw * charge
        return mixed * sigmoid(mixed)

    center = mm(
        w_center_t, hidden(mine[4:5, :], mine[3:4, :], cw, kind_row).astype(bf16)
    )
    center2 = jnp.concatenate([center, center], axis=1)
    kind_row2 = jnp.concatenate([kind_row, kind_row], axis=1)

    def wide(packed, c):
        return jnp.concatenate([packed[2 * c : 2 * c + 1, :], packed[2 * c + 1 : 2 * c + 2, :]], axis=1)

    def basis(c):
        spread = wide(dist, c) - centres
        return spread, jnp.exp(-2.0 * spread * spread)

    for c in range(4):
        at = slice(256 * c, 256 * c + 256)
        hid = hidden(wide(far_s, c), wide(far_q, c), cw2, kind_row2)
        _, rb = basis(c)
        rb_high = rb.astype(bf16).astype(f32)
        rhs = jnp.concatenate([hid, rb_high, rb_high, rb - rb_high, jnp.zeros_like(rb)], axis=0)
        pair = mm(w_pair, rhs.astype(bf16)) + center2
        sig = sigmoid(pair)
        act = pair * sig
        ds1_ref[:, at] = sig + act * (1.0 - sig)
        second = mm(w_two_t, act.astype(bf16))
        sig = sigmoid(second)
        latent = second * sig
        ds2_ref[:, at] = sig + latent * (1.0 - sig)
        lat_ref[:, at] = latent
        latent_bf = latent.astype(bf16)
        lb_ref[:, at] = latent_bf
        both = mm(w_ec_t, latent_bf)
        er_ref[:, at] = both[:64]
        ch_ref[:, at] = both[64:]

    def row_of(packed, r):
        return packed[r : r + 1, :]

    def lanes(r):
        return slice(128 * r, 128 * r + 128)

    group_of = [0, 1, 1, 1, 2, 2, 2, 2, 2]
    weighted = [None] + [h * weight for h in harm[1:]]
    for m in range(9):
        scale = weight if m == 0 else weighted[m]
        total = er_ref[:, lanes(0)] * row_of(scale, 0)
        for r in range(1, 8):
            total = total + er_ref[:, lanes(r)] * row_of(scale, r)
        s_ref[m] = 0.25 * half_turn(total)

    def double(value):
        return jnp.concatenate([value, value], axis=1)

    def keep_row(index, c, value):
        rows_ref[index, 2 * c : 2 * c + 1, :] = value[:, :128]
        rows_ref[index, 2 * c + 1 : 2 * c + 2, :] = value[:, 128:]

    for c in range(4):
        at = slice(256 * c, 256 * c + 256)
        channel = ch_ref[:, at]
        grouped = [double(s_ref[0]), None, None]
        for m in range(1, 9):
            term = double(s_ref[m]) * wide(harm[m], c)
            g = group_of[m]
            grouped[g] = term if grouped[g] is None else grouped[g] + term
        scalars = [(g * channel).astype(bf16) for g in grouped]
        joined = jnp.concatenate([lb_ref[:, at]] + scalars, axis=0)
        update = mm(w_lat_t, joined)
        sig = sigmoid(update)
        act = update * sig
        out_bf = (lat_ref[:, at] + act).astype(bf16)
        keep_row(0, c, mm(w_out_row, out_bf)[0:1])
        d_update = (wo2 * wide(weight, c) * (sig + act * (1.0 - sig))).astype(bf16)
        du_ref[:, at] = d_update
        d_scal = mm(w_scal, d_update)
        d_grouped = []
        d_channel = None
        for g in range(3):
            part = d_scal[64 * g : 64 * g + 64]
            term = part * grouped[g]
            d_channel = term if d_channel is None else d_channel + term
            d_grouped.append(part * channel)
            dg_ref[g, :, at] = d_grouped[g]
        dch_ref[:, at] = d_channel.astype(bf16)
        for m in range(1, 9):
            keep_row(m, c, jnp.sum(d_grouped[group_of[m]] * double(s_ref[m]), axis=0, keepdims=True))

    for m in range(9):
        g = group_of[m]
        total = None
        for r in range(8):
            term = dg_ref[g, :, lanes(r)]
            if m > 0:
                term = term * row_of(harm[m], r)
            total = term if total is None else total + term
        dsum_ref[m] = 0.25 * half_turn(total)

    for c in range(4):
        at = slice(256 * c, 256 * c + 256)
        raw = er_ref[:, at]
        w_row = wide(weight, c)
        d_env = double(dsum_ref[0])
        for m in range(1, 9):
            back = double(dsum_ref[m])
            d_env = d_env + back * wide(harm[m], c)
            keep_row(8 + m, c, jnp.sum(raw * back, axis=0, keepdims=True))
        keep_row(17, c, jnp.sum(raw * d_env, axis=0, keepdims=True))
        d_joined = jnp.concatenate(
            [du_ref[:, at], (d_env * w_row).astype(bf16), dch_ref[:, at]], axis=0
        )
        d_latent = mm(w_back, d_joined) + wo2 * w_row
        d_second = (d_latent * ds2_ref[:, at]).astype(bf16)
        d_pair = mm(w_two_ref[...], d_second) * ds1_ref[:, at]
        high = d_pair.astype(bf16)
        low = (d_pair - high.astype(f32)).astype(bf16)
        first = mm(w_rad, high)
        d_basis = first[0:8] + first[8:16] + mm(w_rad, low)[0:8]
        spread, rb = basis(c)
        keep_row(18, c, jnp.sum(d_basis * rb * spread, axis=0, keepdims=True) * -4.0)

    energy = jnp.sum(rows_ref[0] * weight, axis=0, keepdims=True)
    energy_ref[...] = half_turn(energy)[:, :64]
    d_h = [None] + [rows_ref[m] + weight * rows_ref[8 + m] for m in range(1, 9)]
    g_x = d_h[1] + y * d_h[4] + z * d_h[6] + 2.0 * x * (d_h[7] - d_h[8])
    g_y = d_h[2] + x * d_h[4] + z * d_h[5] - 2.0 * y * (d_h[7] + d_h[8])
    g_z = d_h[3] + y * d_h[5] + x * d_h[6] + 4.0 * z * d_h[8]
    d_weight = rows_ref[0] + rows_ref[17]
    d_dist = (
        rows_ref[18]
        - inv * (g_x * x + g_y * y + g_z * z)
        - d_weight * weight * dist * (1.0 / 16.0)
    )
    e_x = g_x * inv + d_dist * x
    e_y = g_y * inv + d_dist * y
    e_z = g_z * inv + d_dist * z

    home_u = centre_of(odd_x, BACK[0][0])
    home_v = centre_of(odd_y, BACK[0][1])
    u = home_u + step_x
    v = home_v + step_y
    target = ((u // 2) * 2 + v // 2) * 4 + (u % 2) * 2 + v % 2
    atom_row = lax.broadcasted_iota(jnp.int32, (64, 128), 0)
    pairs_row = lax.broadcasted_iota(jnp.int32, (8, 128), 0)
    part_row = lax.rem(pairs_row, 4)
    left, right = [], []
    for r in range(8):
        mixed = jnp.where(
            part_row == 0,
            row_of(e_x, r),
            jnp.where(part_row == 1, row_of(e_y, r), jnp.where(part_row == 2, row_of(e_z, r), 0.0)),
        )
        high = mixed.astype(bf16).astype(f32)
        low = mixed - high
        goal = jnp.broadcast_to(row_of(target, r), (8, 128)) - jnp.where(pairs_row >= 4, 1, 0)
        stack = [jnp.where(goal == 2 * i, high, 0.0) for i in range(8)]
        stack += [jnp.where(goal == 2 * i, low, 0.0) for i in range(8)]
        left.append(jnp.concatenate(stack, axis=0).astype(bf16))
        right.append(jnp.where(atom_row == row_of(atom, r), 1.0, 0.0).astype(bf16))
    far = lax.dot_general(
        jnp.concatenate(left, axis=1),
        jnp.concatenate(right, axis=1),
        (((1,), (1,)), ((), ())),
        preferred_element_type=f32,
    )
    far = far[:64] + far[64:]
    near = jnp.concatenate(
        [half_turn(jnp.sum(e, axis=0, keepdims=True))[:, :64] for e in (e_x, e_y, e_z)]
        + [jnp.zeros((1, 64), f32)],
        axis=0,
    )
    home = (home_u // 2 * 2 + home_v // 2) * 4 + home_u % 2 * 2 + home_v % 2
    grad_ref[...] = jnp.zeros_like(grad_ref)
    for i in range(16):
        here = far[4 * i : 4 * i + 4] - jnp.where(home == i, near, 0.0)
        grad_ref[i // 4, 8 * (i % 4) : 8 * (i % 4) + 4, 0:64] = here


vmem = pl.BlockSpec(memory_space=pltpu.VMEM)


def edges(*operands):
    return pl.pallas_call(
        edge_kernel,
        out_shape=(
            jax.ShapeDtypeStruct((4, 32, 128), f32),
            jax.ShapeDtypeStruct((1, 64), f32),
        ),
        in_specs=[vmem] * len(operands),
        out_specs=(vmem, vmem),
        scratch_shapes=[
            pltpu.VMEM((128, 1024), f32),
            pltpu.VMEM((128, 1024), f32),
            pltpu.VMEM((128, 1024), f32),
            pltpu.VMEM((128, 1024), bf16),
            pltpu.VMEM((64, 1024), f32),
            pltpu.VMEM((64, 1024), f32),
            pltpu.VMEM((9, 64, 128), f32),
            pltpu.VMEM((3, 64, 1024), f32),
            pltpu.VMEM((128, 1024), bf16),
            pltpu.VMEM((64, 1024), bf16),
            pltpu.VMEM((9, 64, 128), f32),
            pltpu.VMEM((19, 8, 128), f32),
        ],
        compiler_params=pltpu.CompilerParams(vmem_limit_bytes=16 * 1024 * 1024),
        name="edges",
    )(*operands)


def local(
    positions,
    species,
    charges,
    neighbours,
    counts,
    send_list,
    species_table,
    charge_weight,
    w_center,
    w_neigh,
    w_radial,
    w_two,
    w_env,
    w_tensor,
    w_latent,
    w_out,
):
    first, whole, small = pl.pallas_call(
        pack_kernel,
        out_shape=(
            jax.ShapeDtypeStruct((4, 8, 128), f32),
            jax.ShapeDtypeStruct((24, 64), jnp.int32),
            jax.ShapeDtypeStruct((24, 128), f32),
        ),
        in_specs=[vmem] * 10,
        out_specs=(vmem, vmem, vmem),
        compiler_params=pltpu.CompilerParams(vmem_limit_bytes=1024 * 1024),
        name="pack",
    )(
        positions.reshape(3, 1, 64),
        charges[0],
        species[0],
        send_list[0],
        neighbours[0, 0],
        counts[0],
        species_table,
        charge_weight[None],
        w_radial,
        w_out[None],
    )
    four = swap(first, FORTH[0]).reshape(32, 128)
    blocks = swap(jnp.broadcast_to(four[None], (4, 32, 128)), FORTH[1])
    grads, energy = edges(
        blocks,
        whole,
        small,
        w_center,
        w_neigh,
        w_two,
        w_env[0].T,
        w_tensor[0].T,
        w_latent[0],
    )
    sums = jnp.sum(swap(grads, BACK[0]), axis=0).reshape(4, 8, 128)
    forces = pl.pallas_call(
        force_kernel,
        out_shape=jax.ShapeDtypeStruct((3, 1, 64), f32),
        in_specs=[vmem],
        out_specs=vmem,
        compiler_params=pltpu.CompilerParams(vmem_limit_bytes=1024 * 1024),
        name="forces",
    )(swap(sums, BACK[1]))
    return (energy[None], forces.reshape(1, 1, 3, 64))


def solution(mesh):
    return jax.shard_map(
        local,
        mesh=mesh,
        in_specs=(
            P("gx", "yz", None, None),
            P("gx", "yz", None),
            P("gx", "yz", None),
            P("gx", "yz", None, None),
            P("gx", "yz", None),
            P("gx", "yz", None),
            P(),
            P(),
            P(),
            P(),
            P(),
            P(),
            P(),
            P(),
            P(),
            P(),
        ),
        out_specs=(P("gx", "yz", None), P("gx", "yz", None, None)),
        check_vma=False,
    )
```

```python
import jax
import jax.numpy as jnp
from jax import lax
from jax.experimental import pallas as pl
from jax.experimental.pallas import tpu as pltpu
from jax.sharding import PartitionSpec as P

box_side = 3.0
f32 = jnp.float32
bf16 = jnp.bfloat16


FORTH = ((0, 0), (1, 1))
BACK = ((0, 0), (1, 1))


def groups_of(pairing):
    slabs, columns = lax.axis_size("gx"), lax.axis_size("yz")
    return [
        [
            (2 * m + pairing[0] + a) % slabs * columns + (2 * n + pairing[1] + b) % columns
            for a in (0, 1)
            for b in (0, 1)
        ]
        for m in range(slabs // 2)
        for n in range(columns // 2)
    ]


def swap(value, pairing):
    return lax.all_to_all(value, ("gx", "yz"), 0, 0, axis_index_groups=groups_of(pairing))


def centre_of(odd, outer):
    return 2 - odd if outer else 1 + odd


def halves(value):
    high = value.astype(bf16).astype(f32)
    return high, value - high


def turned(value):
    return value.astype(f32).T.astype(bf16)


def mm(a, b):
    return jnp.dot(a, b, preferred_element_type=f32)


span = 8


def repeat(value, axis=1):
    return jnp.concatenate([value] * span, axis=axis)


def half_turn(x):
    return x + pltpu.roll(x, 64, 1)


def sigmoid(x):
    return 0.5 * jnp.tanh(0.5 * x) + 0.5


def pack_kernel(pos_ref, charge_ref, kind_ref, send_ref, out_ref):
    out_ref[...] = jnp.zeros_like(out_ref)
    for k in range(4):
        for i in range(3):
            out_ref[k, i : i + 1, 0:64] = pos_ref[i]
        out_ref[k, 3:4, 0:64] = charge_ref[...]
        out_ref[k, 4:5, 0:64] = kind_ref[...].astype(f32)
        out_ref[k, 5:6, 0:56] = send_ref[...].astype(f32)


def spread_kernel(four_ref, nb_ref, count_ref, out_ref, whole_ref):
    for k in range(4):
        out_ref[k] = four_ref[...]
    whole_ref[0:16, :] = nb_ref[...]
    whole_ref[16:17, :] = count_ref[...]


def force_kernel(parts_ref, out_ref):
    total = parts_ref[0] + parts_ref[1] + parts_ref[2] + parts_ref[3]
    for i in range(3):
        out_ref[i] = -total[i : i + 1, 0:64]


def edge_kernel(
    blocks_ref,
    whole_ref,
    table_ref,
    charge_weight_ref,
    w_center_ref,
    w_neigh_ref,
    w_radial_ref,
    w_two_ref,
    w_env_t_ref,
    w_tensor_t_ref,
    w_latent_ref,
    w_out_ref,
    grad_ref,
    energy_ref,
    lat_ref,
    ds1_ref,
    ds2_ref,
    lb_ref,
    er_ref,
    ch_ref,
    s_ref,
    dg_ref,
    du_ref,
    dch_ref,
    dsum_ref,
    rows_ref,
    table8_ref,
):
    table8_ref[...] = jnp.zeros_like(table8_ref)
    table8_ref[0:6, :] = table_ref[...]
    w_center_t = turned(w_center_ref[...])
    w_neigh_t = turned(w_neigh_ref[...])
    w_two_t = turned(w_two_ref[...])
    w_lat_t = jnp.concatenate(
        [turned(w_latent_ref[0:128, :]), turned(w_latent_ref[128:256, :]), turned(w_latent_ref[256:320, :])],
        axis=1,
    )
    w_ec_t = jnp.concatenate([w_env_t_ref[...], w_tensor_t_ref[...]], axis=0)
    w_back = jnp.concatenate([w_latent_ref[0:128, :], turned(w_ec_t)], axis=1)
    w_scal = w_latent_ref[128:320, :]
    w_out = w_out_ref[...].astype(f32)
    w_out_row = jnp.broadcast_to(w_out, (16, 128)).astype(bf16)
    wo = jnp.broadcast_to(w_out, (128, 128)).T
    kind_high, rest = halves(table8_ref[...])
    kind_mid, kind_low = halves(rest)
    rad_high, rad_low = halves(w_radial_ref[...])
    none = jnp.zeros((8, 128), f32)
    small = jnp.concatenate(
        [rad_high, rad_low, rad_high, none, kind_high, kind_mid, kind_low, none, jnp.zeros((64, 128), f32)],
        axis=0,
    ).T.astype(bf16)
    w_pair = jnp.concatenate([w_neigh_t, small[:, 0:32]], axis=1)
    w_kind = small[:, 32:64]
    w_rad = jnp.concatenate([rad_high, rad_low], axis=0).astype(bf16)
    cw = jnp.broadcast_to(charge_weight_ref[...], (128, 128)).T

    odd_x = lax.rem(lax.axis_index("gx"), 2)
    odd_y = lax.rem(lax.axis_index("yz"), 2)

    def block(b):
        u = centre_of(odd_x, FORTH[1][0]) + (b // 3 - 1)
        v = centre_of(odd_y, FORTH[1][1]) + (b % 3 - 1)
        far = (u // 2) * 2 + v // 2
        near = (u % 2) * 2 + v % 2
        return blocks_ref[far, pl.ds(pl.multiple_of(near * 8, 8), 8), :]

    tables = [block(b) for b in range(9)]

    ids = jnp.concatenate([whole_ref[0:8, :], whole_ref[8:16, :]], axis=1)
    count = jnp.concatenate([whole_ref[16:17, :], whole_ref[16:17, :]], axis=1)
    row = lax.broadcasted_iota(jnp.int32, (8, 128), 0)
    lane = lax.broadcasted_iota(jnp.int32, (8, 128), 1)
    slot = row + jnp.where(lane >= 64, 8, 0)
    live = jnp.where(slot < count, 1.0, 0.0)
    own = ids < 64
    beyond = ids - 64
    blk = jnp.zeros_like(ids)
    for b in range(1, 9):
        blk = blk + jnp.where(beyond >= 56 * b, 1, 0)
    place = jnp.where(own, ids, beyond - 56 * blk)
    blk = jnp.where(own, 4, blk)

    def pick(which, index, start):
        out = start
        for b in range(9):
            table = jnp.broadcast_to(tables[b][which : which + 1, :], (8, 128))
            value = jnp.take_along_axis(table, index, axis=1, mode="promise_in_bounds")
            out = jnp.where(blk == b, value, out)
        return out

    listed = pick(5, place, jnp.zeros((8, 128), f32)).astype(jnp.int32)
    atom = jnp.where(own, ids, listed)
    zero = jnp.zeros((8, 128), f32)
    far_x, far_y, far_z, far_q, far_s = [pick(i, atom, zero) for i in range(5)]
    step_x = jnp.where(blk >= 6, 1, jnp.where(blk >= 3, 0, -1))
    step_y = blk - 3 * (step_x + 1) - 1
    mine = half_turn(tables[4])
    off_x = far_x + box_side * step_x.astype(f32) - mine[0:1, :]
    off_y = far_y + box_side * step_y.astype(f32) - mine[1:2, :]
    off_z = far_z - mine[2:3, :]
    square = off_x * off_x + off_y * off_y + off_z * off_z + 1.0
    dist = jnp.sqrt(square)
    inv = 1.0 / dist
    x, y, z = off_x * inv, off_y * inv, off_z * inv
    harm = [
        None,
        x,
        y,
        z,
        x * y,
        y * z,
        x * z,
        x * x - y * y,
        2.0 * z * z - x * x - y * y,
    ]
    weight = jnp.exp(square * (-1.0 / 32.0)) * live

    kind_row = lax.broadcasted_iota(jnp.int32, (8, 128), 0).astype(f32)
    cw2 = repeat(cw)
    wo2 = repeat(wo)
    centres = 1.0 + lax.broadcasted_iota(jnp.int32, (8, 128 * span), 0).astype(f32)

    def hidden(kind, charge, wide_cw, wide_row):
        onehot = jnp.where(kind == wide_row, 1.0, 0.0)
        pad = jnp.zeros_like(onehot)
        rhs = jnp.concatenate([onehot, onehot, onehot, pad], axis=0).astype(bf16)
        mixed = mm(w_kind, rhs) + wide_cw * charge
        return mixed * sigmoid(mixed)

    center = mm(
        w_center_t, hidden(mine[4:5, :], mine[3:4, :], cw, kind_row).astype(bf16)
    )
    center2 = repeat(center)
    kind_row2 = repeat(kind_row)

    def wide(packed, c):
        return jnp.concatenate([packed[r : r + 1, :] for r in range(span * c, span * c + span)], axis=1)

    def basis(c):
        spread = wide(dist, c) - centres
        return spread, jnp.exp(-2.0 * spread * spread)

    for c in range(8 // span):
        at = slice(128 * span * c, 128 * span * (c + 1))
        hid = hidden(wide(far_s, c), wide(far_q, c), cw2, kind_row2)
        _, rb = basis(c)
        rb_high = rb.astype(bf16).astype(f32)
        rhs = jnp.concatenate([hid, rb_high, rb_high, rb - rb_high, jnp.zeros_like(rb)], axis=0)
        pair = mm(w_pair, rhs.astype(bf16)) + center2
        sig = sigmoid(pair)
        act = pair * sig
        ds1_ref[:, at] = sig + act * (1.0 - sig)
        second = mm(w_two_t, act.astype(bf16))
        sig = sigmoid(second)
        latent = second * sig
        ds2_ref[:, at] = sig + latent * (1.0 - sig)
        lat_ref[:, at] = latent
        latent_bf = latent.astype(bf16)
        lb_ref[:, at] = latent_bf
        both = mm(w_ec_t, latent_bf)
        er_ref[:, at] = both[:64]
        ch_ref[:, at] = both[64:]

    def row_of(packed, r):
        return packed[r : r + 1, :]

    def lanes(r):
        return slice(128 * r, 128 * r + 128)

    group_of = [0, 1, 1, 1, 2, 2, 2, 2, 2]
    weighted = [None] + [h * weight for h in harm[1:]]
    for m in range(9):
        scale = weight if m == 0 else weighted[m]
        total = er_ref[:, lanes(0)] * row_of(scale, 0)
        for r in range(1, 8):
            total = total + er_ref[:, lanes(r)] * row_of(scale, r)
        s_ref[m] = 0.25 * half_turn(total)

    def keep_row(index, c, value):
        for i in range(span):
            rows_ref[index, span * c + i : span * c + i + 1, :] = value[:, 128 * i : 128 * i + 128]

    for c in range(8 // span):
        at = slice(128 * span * c, 128 * span * (c + 1))
        channel = ch_ref[:, at]
        grouped = [repeat(s_ref[0]), None, None]
        for m in range(1, 9):
            term = repeat(s_ref[m]) * wide(harm[m], c)
            g = group_of[m]
            grouped[g] = term if grouped[g] is None else grouped[g] + term
        scalars = [(g * channel).astype(bf16) for g in grouped]
        joined = jnp.concatenate([lb_ref[:, at]] + scalars, axis=0)
        update = mm(w_lat_t, joined)
        sig = sigmoid(update)
        act = update * sig
        out_bf = (lat_ref[:, at] + act).astype(bf16)
        keep_row(0, c, mm(w_out_row, out_bf)[0:1])
        d_update = (wo2 * wide(weight, c) * (sig + act * (1.0 - sig))).astype(bf16)
        du_ref[:, at] = d_update
        d_scal = mm(w_scal, d_update)
        d_grouped = []
        d_channel = None
        for g in range(3):
            part = d_scal[64 * g : 64 * g + 64]
            term = part * grouped[g]
            d_channel = term if d_channel is None else d_channel + term
            d_grouped.append(part * channel)
            dg_ref[g, :, at] = d_grouped[g]
        dch_ref[:, at] = d_channel.astype(bf16)
        for m in range(1, 9):
            keep_row(m, c, jnp.sum(d_grouped[group_of[m]] * repeat(s_ref[m]), axis=0, keepdims=True))

    for m in range(9):
        g = group_of[m]
        total = None
        for r in range(8):
            term = dg_ref[g, :, lanes(r)]
            if m > 0:
                term = term * row_of(harm[m], r)
            total = term if total is None else total + term
        dsum_ref[m] = 0.25 * half_turn(total)

    for c in range(8 // span):
        at = slice(128 * span * c, 128 * span * (c + 1))
        raw = er_ref[:, at]
        w_row = wide(weight, c)
        d_env = repeat(dsum_ref[0])
        for m in range(1, 9):
            back = repeat(dsum_ref[m])
            d_env = d_env + back * wide(harm[m], c)
            keep_row(8 + m, c, jnp.sum(raw * back, axis=0, keepdims=True))
        keep_row(17, c, jnp.sum(raw * d_env, axis=0, keepdims=True))
        d_joined = jnp.concatenate(
            [du_ref[:, at], (d_env * w_row).astype(bf16), dch_ref[:, at]], axis=0
        )
        d_latent = mm(w_back, d_joined) + wo2 * w_row
        d_second = (d_latent * ds2_ref[:, at]).astype(bf16)
        d_pair = mm(w_two_ref[...], d_second) * ds1_ref[:, at]
        high = d_pair.astype(bf16)
        low = (d_pair - high.astype(f32)).astype(bf16)
        first = mm(w_rad, high)
        d_basis = first[0:8] + first[8:16] + mm(w_rad, low)[0:8]
        spread, rb = basis(c)
        keep_row(18, c, jnp.sum(d_basis * rb * spread, axis=0, keepdims=True) * -4.0)

    energy = jnp.sum(rows_ref[0] * weight, axis=0, keepdims=True)
    energy_ref[...] = half_turn(energy)[:, :64]
    d_h = [None] + [rows_ref[m] + weight * rows_ref[8 + m] for m in range(1, 9)]
    g_x = d_h[1] + y * d_h[4] + z * d_h[6] + 2.0 * x * (d_h[7] - d_h[8])
    g_y = d_h[2] + x * d_h[4] + z * d_h[5] - 2.0 * y * (d_h[7] + d_h[8])
    g_z = d_h[3] + y * d_h[5] + x * d_h[6] + 4.0 * z * d_h[8]
    d_weight = rows_ref[0] + rows_ref[17]
    d_dist = (
        rows_ref[18]
        - inv * (g_x * x + g_y * y + g_z * z)
        - d_weight * weight * dist * (1.0 / 16.0)
    )
    e_x = g_x * inv + d_dist * x
    e_y = g_y * inv + d_dist * y
    e_z = g_z * inv + d_dist * z

    home_u = centre_of(odd_x, BACK[0][0])
    home_v = centre_of(odd_y, BACK[0][1])
    u = home_u + step_x
    v = home_v + step_y
    target = ((u // 2) * 2 + v // 2) * 4 + (u % 2) * 2 + v % 2
    atom_row = lax.broadcasted_iota(jnp.int32, (64, 128), 0)
    pairs_row = lax.broadcasted_iota(jnp.int32, (8, 128), 0)
    part_row = lax.rem(pairs_row, 4)
    left, right = [], []
    for r in range(8):
        mixed = jnp.where(
            part_row == 0,
            row_of(e_x, r),
            jnp.where(part_row == 1, row_of(e_y, r), jnp.where(part_row == 2, row_of(e_z, r), 0.0)),
        )
        high = mixed.astype(bf16).astype(f32)
        low = mixed - high
        goal = jnp.broadcast_to(row_of(target, r), (8, 128)) - jnp.where(pairs_row >= 4, 1, 0)
        stack = [jnp.where(goal == 2 * i, high, 0.0) for i in range(8)]
        stack += [jnp.where(goal == 2 * i, low, 0.0) for i in range(8)]
        left.append(jnp.concatenate(stack, axis=0).astype(bf16))
        right.append(jnp.where(atom_row == row_of(atom, r), 1.0, 0.0).astype(bf16))
    far = lax.dot_general(
        jnp.concatenate(left, axis=1),
        jnp.concatenate(right, axis=1),
        (((1,), (1,)), ((), ())),
        preferred_element_type=f32,
    )
    far = far[:64] + far[64:]
    near = jnp.concatenate(
        [half_turn(jnp.sum(e, axis=0, keepdims=True))[:, :64] for e in (e_x, e_y, e_z)]
        + [jnp.zeros((1, 64), f32)],
        axis=0,
    )
    home = (home_u // 2 * 2 + home_v // 2) * 4 + home_u % 2 * 2 + home_v % 2
    grad_ref[...] = jnp.zeros_like(grad_ref)
    for i in range(16):
        here = far[4 * i : 4 * i + 4] - jnp.where(home == i, near, 0.0)
        grad_ref[i // 4, 8 * (i % 4) : 8 * (i % 4) + 4, 0:64] = here


vmem = pl.BlockSpec(memory_space=pltpu.VMEM)


def edges(*operands):
    return pl.pallas_call(
        edge_kernel,
        out_shape=(
            jax.ShapeDtypeStruct((4, 32, 128), f32),
            jax.ShapeDtypeStruct((1, 64), f32),
        ),
        in_specs=[vmem] * len(operands),
        out_specs=(vmem, vmem),
        scratch_shapes=[
            pltpu.VMEM((128, 1024), f32),
            pltpu.VMEM((128, 1024), f32),
            pltpu.VMEM((128, 1024), f32),
            pltpu.VMEM((128, 1024), bf16),
            pltpu.VMEM((64, 1024), f32),
            pltpu.VMEM((64, 1024), f32),
            pltpu.VMEM((9, 64, 128), f32),
            pltpu.VMEM((3, 64, 1024), f32),
            pltpu.VMEM((128, 1024), bf16),
            pltpu.VMEM((64, 1024), bf16),
            pltpu.VMEM((9, 64, 128), f32),
            pltpu.VMEM((19, 8, 128), f32),
            pltpu.VMEM((8, 128), f32),
        ],
        compiler_params=pltpu.CompilerParams(vmem_limit_bytes=16 * 1024 * 1024),
        name="edges",
    )(*operands)


def local(
    positions,
    species,
    charges,
    neighbours,
    counts,
    send_list,
    species_table,
    charge_weight,
    w_center,
    w_neigh,
    w_radial,
    w_two,
    w_env,
    w_tensor,
    w_latent,
    w_out,
):
    first = pl.pallas_call(
        pack_kernel,
        out_shape=jax.ShapeDtypeStruct((4, 8, 128), f32),
        in_specs=[vmem] * 4,
        out_specs=vmem,
        compiler_params=pltpu.CompilerParams(vmem_limit_bytes=1024 * 1024),
        name="pack",
    )(positions.reshape(3, 1, 64), charges[0], species[0], send_list[0])
    second, whole = pl.pallas_call(
        spread_kernel,
        out_shape=(
            jax.ShapeDtypeStruct((4, 32, 128), f32),
            jax.ShapeDtypeStruct((24, 64), jnp.int32),
        ),
        in_specs=[vmem] * 3,
        out_specs=(vmem, vmem),
        compiler_params=pltpu.CompilerParams(vmem_limit_bytes=1024 * 1024),
        name="spread",
    )(swap(first, FORTH[0]).reshape(32, 128), neighbours[0, 0], counts[0])
    grads, energy = edges(
        swap(second, FORTH[1]),
        whole,
        species_table,
        charge_weight[None],
        w_center,
        w_neigh,
        w_radial,
        w_two,
        w_env[0].T,
        w_tensor[0].T,
        w_latent[0],
        w_out[None],
    )
    sums = jnp.sum(swap(grads, BACK[0]), axis=0).reshape(4, 8, 128)
    forces = pl.pallas_call(
        force_kernel,
        out_shape=jax.ShapeDtypeStruct((3, 1, 64), f32),
        in_specs=[vmem],
        out_specs=vmem,
        compiler_params=pltpu.CompilerParams(vmem_limit_bytes=1024 * 1024),
        name="forces",
    )(swap(sums, BACK[1]))
    return (energy[None], forces.reshape(1, 1, 3, 64))


def solution(mesh):
    return jax.shard_map(
        local,
        mesh=mesh,
        in_specs=(
            P("gx", "yz", None, None),
            P("gx", "yz", None),
            P("gx", "yz", None),
            P("gx", "yz", None, None),
            P("gx", "yz", None),
            P("gx", "yz", None),
            P(),
            P(),
            P(),
            P(),
            P(),
            P(),
            P(),
            P(),
            P(),
            P(),
        ),
        out_specs=(P("gx", "yz", None), P("gx", "yz", None, None)),
        check_vma=False,
    )
```

```python
import jax
import jax.numpy as jnp
from jax import lax
from jax.experimental import pallas as pl
from jax.experimental.pallas import tpu as pltpu
from jax.sharding import PartitionSpec as P

box_side = 3.0
f32 = jnp.float32
bf16 = jnp.bfloat16


FORTH = ((0, 0), (1, 1))
BACK = ((0, 0), (1, 1))


def groups_of(pairing):
    slabs, columns = lax.axis_size("gx"), lax.axis_size("yz")
    return [
        [
            (2 * m + pairing[0] + a) % slabs * columns + (2 * n + pairing[1] + b) % columns
            for a in (0, 1)
            for b in (0, 1)
        ]
        for m in range(slabs // 2)
        for n in range(columns // 2)
    ]


def swap(value, pairing):
    return lax.all_to_all(value, ("gx", "yz"), 0, 0, axis_index_groups=groups_of(pairing))


def centre_of(odd, outer):
    return 2 - odd if outer else 1 + odd


def halves(value):
    high = value.astype(bf16).astype(f32)
    return high, value - high


def turned(value):
    return value.astype(f32).T.astype(bf16)


def mm(a, b):
    return jnp.dot(a, b, preferred_element_type=f32)


span = 8


def repeat(value, axis=1):
    return jnp.concatenate([value] * span, axis=axis)


def half_turn(x):
    return x + pltpu.roll(x, 64, 1)


def sigmoid(x):
    return 0.5 * jnp.tanh(0.5 * x) + 0.5


def pack_kernel(pos_ref, charge_ref, kind_ref, send_ref, out_ref):
    out_ref[...] = jnp.zeros_like(out_ref)
    code = (kind_ref[:, 0:56] + 8 * send_ref[...]).astype(f32)
    for k in range(4):
        out_ref[k, 0:1, :] = jnp.concatenate([pos_ref[0], pos_ref[1]], axis=1)
        out_ref[k, 1:2, :] = jnp.concatenate([pos_ref[2], charge_ref[...]], axis=1)
        out_ref[k, 2:3, 0:64] = kind_ref[...].astype(f32)
        out_ref[k, 2:3, 0:56] = code


def spread_kernel(four_ref, nb_ref, count_ref, out_ref, whole_ref):
    for k in range(4):
        out_ref[k] = four_ref[...]
    whole_ref[0:16, :] = nb_ref[...]
    whole_ref[16:17, :] = count_ref[...]


def force_kernel(parts_ref, out_ref):
    total = parts_ref[0] + parts_ref[1] + parts_ref[2] + parts_ref[3]
    out_ref[0] = -total[0:1, 0:64]
    out_ref[1] = -pltpu.roll(total, 64, 1)[0:1, 0:64]
    out_ref[2] = -total[1:2, 0:64]


def edge_kernel(
    blocks_ref,
    whole_ref,
    table_ref,
    charge_weight_ref,
    w_center_ref,
    w_neigh_ref,
    w_radial_ref,
    w_two_ref,
    w_env_t_ref,
    w_tensor_t_ref,
    w_latent_ref,
    w_out_ref,
    grad_ref,
    energy_ref,
    lat_ref,
    ds1_ref,
    ds2_ref,
    lb_ref,
    er_ref,
    ch_ref,
    s_ref,
    dg_ref,
    du_ref,
    dch_ref,
    dsum_ref,
    rows_ref,
    table8_ref,
):
    table8_ref[...] = jnp.zeros_like(table8_ref)
    table8_ref[0:6, :] = table_ref[...]
    w_center_t = turned(w_center_ref[...])
    w_neigh_t = turned(w_neigh_ref[...])
    w_two_t = turned(w_two_ref[...])
    w_lat_t = jnp.concatenate(
        [turned(w_latent_ref[0:128, :]), turned(w_latent_ref[128:256, :]), turned(w_latent_ref[256:320, :])],
        axis=1,
    )
    w_ec_t = jnp.concatenate([w_env_t_ref[...], w_tensor_t_ref[...]], axis=0)
    w_back = jnp.concatenate([w_latent_ref[0:128, :], turned(w_ec_t)], axis=1)
    w_scal = w_latent_ref[128:320, :]
    w_out = w_out_ref[...].astype(f32)
    w_out_row = jnp.broadcast_to(w_out, (16, 128)).astype(bf16)
    wo = jnp.broadcast_to(w_out, (128, 128)).T
    kind_high, rest = halves(table8_ref[...])
    kind_mid, kind_low = halves(rest)
    rad_high, rad_low = halves(w_radial_ref[...])
    none = jnp.zeros((8, 128), f32)
    small = jnp.concatenate(
        [rad_high, rad_low, rad_high, none, kind_high, kind_mid, kind_low, none, jnp.zeros((64, 128), f32)],
        axis=0,
    ).T.astype(bf16)
    w_pair = jnp.concatenate([w_neigh_t, small[:, 0:32]], axis=1)
    w_kind = small[:, 32:64]
    w_rad = jnp.concatenate([rad_high, rad_low], axis=0).astype(bf16)
    cw = jnp.broadcast_to(charge_weight_ref[...], (128, 128)).T

    odd_x = lax.rem(lax.axis_index("gx"), 2)
    odd_y = lax.rem(lax.axis_index("yz"), 2)

    def block(b):
        u = centre_of(odd_x, FORTH[1][0]) + (b // 3 - 1)
        v = centre_of(odd_y, FORTH[1][1]) + (b % 3 - 1)
        far = (u // 2) * 2 + v // 2
        near = (u % 2) * 2 + v % 2
        return [blocks_ref[far, pl.ds(near * 8 + i, 1), :] for i in range(3)]

    tables = [block(b) for b in range(9)]

    ids = jnp.concatenate([whole_ref[0:8, :], whole_ref[8:16, :]], axis=1)
    count = jnp.concatenate([whole_ref[16:17, :], whole_ref[16:17, :]], axis=1)
    row = lax.broadcasted_iota(jnp.int32, (8, 128), 0)
    lane = lax.broadcasted_iota(jnp.int32, (8, 128), 1)
    slot = row + jnp.where(lane >= 64, 8, 0)
    live = jnp.where(slot < count, 1.0, 0.0)
    own = ids < 64
    beyond = ids - 64
    blk = jnp.zeros_like(ids)
    for b in range(1, 9):
        blk = blk + jnp.where(beyond >= 56 * b, 1, 0)
    place = jnp.where(own, ids, beyond - 56 * blk)
    blk = jnp.where(own, 4, blk)

    def pick(which, index, start):
        out = start
        for b in range(9):
            table = jnp.broadcast_to(tables[b][which], (8, 128))
            value = jnp.take_along_axis(table, index, axis=1, mode="promise_in_bounds")
            out = jnp.where(blk == b, value, out)
        return out

    zero = jnp.zeros((8, 128), f32)
    listed = pick(2, place, zero).astype(jnp.int32) // 8
    atom = jnp.where(own, ids, listed)
    far_x = pick(0, atom, zero)
    far_y = pick(0, atom + 64, zero)
    far_z = pick(1, atom, zero)
    far_q = pick(1, atom + 64, zero)
    far_s = (pick(2, atom, zero).astype(jnp.int32) % 8).astype(f32)
    step_x = jnp.where(blk >= 6, 1, jnp.where(blk >= 3, 0, -1))
    step_y = blk - 3 * (step_x + 1) - 1
    lower = lax.broadcasted_iota(jnp.int32, (1, 128), 1) < 64
    mine = [(table, pltpu.roll(table, 64, 1)) for table in tables[4]]
    (own_x, own_y), (own_z, own_q) = [
        (jnp.where(lower, here, there), jnp.where(lower, there, here)) for here, there in mine[:2]
    ]
    own_s = (half_turn(tables[4][2]).astype(jnp.int32) % 8).astype(f32)
    off_x = far_x + box_side * step_x.astype(f32) - own_x
    off_y = far_y + box_side * step_y.astype(f32) - own_y
    off_z = far_z - own_z
    square = off_x * off_x + off_y * off_y + off_z * off_z + 1.0
    dist = jnp.sqrt(square)
    inv = 1.0 / dist
    x, y, z = off_x * inv, off_y * inv, off_z * inv
    harm = [
        None,
        x,
        y,
        z,
        x * y,
        y * z,
        x * z,
        x * x - y * y,
        2.0 * z * z - x * x - y * y,
    ]
    weight = jnp.exp(square * (-1.0 / 32.0)) * live

    kind_row = lax.broadcasted_iota(jnp.int32, (8, 128), 0).astype(f32)
    cw2 = repeat(cw)
    wo2 = repeat(wo)
    centres = 1.0 + lax.broadcasted_iota(jnp.int32, (8, 128 * span), 0).astype(f32)

    def hidden(kind, charge, wide_cw, wide_row):
        onehot = jnp.where(kind == wide_row, 1.0, 0.0)
        pad = jnp.zeros_like(onehot)
        rhs = jnp.concatenate([onehot, onehot, onehot, pad], axis=0).astype(bf16)
        mixed = mm(w_kind, rhs) + wide_cw * charge
        return mixed * sigmoid(mixed)

    center = mm(
        w_center_t, hidden(own_s, own_q, cw, kind_row).astype(bf16)
    )
    center2 = repeat(center)
    kind_row2 = repeat(kind_row)

    def wide(packed, c):
        return jnp.concatenate([packed[r : r + 1, :] for r in range(span * c, span * c + span)], axis=1)

    def basis(c):
        spread = wide(dist, c) - centres
        return spread, jnp.exp(-2.0 * spread * spread)

    for c in range(8 // span):
        at = slice(128 * span * c, 128 * span * (c + 1))
        hid = hidden(wide(far_s, c), wide(far_q, c), cw2, kind_row2)
        _, rb = basis(c)
        rb_high = rb.astype(bf16).astype(f32)
        rhs = jnp.concatenate([hid, rb_high, rb_high, rb - rb_high, jnp.zeros_like(rb)], axis=0)
        pair = mm(w_pair, rhs.astype(bf16)) + center2
        sig = sigmoid(pair)
        act = pair * sig
        ds1_ref[:, at] = sig + act * (1.0 - sig)
        second = mm(w_two_t, act.astype(bf16))
        sig = sigmoid(second)
        latent = second * sig
        ds2_ref[:, at] = sig + latent * (1.0 - sig)
        lat_ref[:, at] = latent
        latent_bf = latent.astype(bf16)
        lb_ref[:, at] = latent_bf
        both = mm(w_ec_t, latent_bf)
        er_ref[:, at] = both[:64]
        ch_ref[:, at] = both[64:]

    def row_of(packed, r):
        return packed[r : r + 1, :]

    def lanes(r):
        return slice(128 * r, 128 * r + 128)

    group_of = [0, 1, 1, 1, 2, 2, 2, 2, 2]
    weighted = [None] + [h * weight for h in harm[1:]]
    for m in range(9):
        scale = weight if m == 0 else weighted[m]
        total = er_ref[:, lanes(0)] * row_of(scale, 0)
        for r in range(1, 8):
            total = total + er_ref[:, lanes(r)] * row_of(scale, r)
        s_ref[m] = 0.25 * half_turn(total)

    def keep_row(index, c, value):
        for i in range(span):
            rows_ref[index, span * c + i : span * c + i + 1, :] = value[:, 128 * i : 128 * i + 128]

    for c in range(8 // span):
        at = slice(128 * span * c, 128 * span * (c + 1))
        channel = ch_ref[:, at]
        grouped = [repeat(s_ref[0]), None, None]
        for m in range(1, 9):
            term = repeat(s_ref[m]) * wide(harm[m], c)
            g = group_of[m]
            grouped[g] = term if grouped[g] is None else grouped[g] + term
        scalars = [(g * channel).astype(bf16) for g in grouped]
        joined = jnp.concatenate([lb_ref[:, at]] + scalars, axis=0)
        update = mm(w_lat_t, joined)
        sig = sigmoid(update)
        act = update * sig
        out_bf = (lat_ref[:, at] + act).astype(bf16)
        keep_row(0, c, mm(w_out_row, out_bf)[0:1])
        d_update = (wo2 * wide(weight, c) * (sig + act * (1.0 - sig))).astype(bf16)
        du_ref[:, at] = d_update
        d_scal = mm(w_scal, d_update)
        d_grouped = []
        d_channel = None
        for g in range(3):
            part = d_scal[64 * g : 64 * g + 64]
            term = part * grouped[g]
            d_channel = term if d_channel is None else d_channel + term
            d_grouped.append(part * channel)
            dg_ref[g, :, at] = d_grouped[g]
        dch_ref[:, at] = d_channel.astype(bf16)
        for m in range(1, 9):
            keep_row(m, c, jnp.sum(d_grouped[group_of[m]] * repeat(s_ref[m]), axis=0, keepdims=True))

    for m in range(9):
        g = group_of[m]
        total = None
        for r in range(8):
            term = dg_ref[g, :, lanes(r)]
            if m > 0:
                term = term * row_of(harm[m], r)
            total = term if total is None else total + term
        dsum_ref[m] = 0.25 * half_turn(total)

    for c in range(8 // span):
        at = slice(128 * span * c, 128 * span * (c + 1))
        raw = er_ref[:, at]
        w_row = wide(weight, c)
        d_env = repeat(dsum_ref[0])
        for m in range(1, 9):
            back = repeat(dsum_ref[m])
            d_env = d_env + back * wide(harm[m], c)
            keep_row(8 + m, c, jnp.sum(raw * back, axis=0, keepdims=True))
        keep_row(17, c, jnp.sum(raw * d_env, axis=0, keepdims=True))
        d_joined = jnp.concatenate(
            [du_ref[:, at], (d_env * w_row).astype(bf16), dch_ref[:, at]], axis=0
        )
        d_latent = mm(w_back, d_joined) + wo2 * w_row
        d_second = (d_latent * ds2_ref[:, at]).astype(bf16)
        d_pair = mm(w_two_ref[...], d_second) * ds1_ref[:, at]
        high = d_pair.astype(bf16)
        low = (d_pair - high.astype(f32)).astype(bf16)
        first = mm(w_rad, high)
        d_basis = first[0:8] + first[8:16] + mm(w_rad, low)[0:8]
        spread, rb = basis(c)
        keep_row(18, c, jnp.sum(d_basis * rb * spread, axis=0, keepdims=True) * -4.0)

    energy = jnp.sum(rows_ref[0] * weight, axis=0, keepdims=True)
    energy_ref[...] = half_turn(energy)[:, :64]
    d_h = [None] + [rows_ref[m] + weight * rows_ref[8 + m] for m in range(1, 9)]
    g_x = d_h[1] + y * d_h[4] + z * d_h[6] + 2.0 * x * (d_h[7] - d_h[8])
    g_y = d_h[2] + x * d_h[4] + z * d_h[5] - 2.0 * y * (d_h[7] + d_h[8])
    g_z = d_h[3] + y * d_h[5] + x * d_h[6] + 4.0 * z * d_h[8]
    d_weight = rows_ref[0] + rows_ref[17]
    d_dist = (
        rows_ref[18]
        - inv * (g_x * x + g_y * y + g_z * z)
        - d_weight * weight * dist * (1.0 / 16.0)
    )
    e_x = g_x * inv + d_dist * x
    e_y = g_y * inv + d_dist * y
    e_z = g_z * inv + d_dist * z

    home_u = centre_of(odd_x, BACK[0][0])
    home_v = centre_of(odd_y, BACK[0][1])
    u = home_u + step_x
    v = home_v + step_y
    target = ((u // 2) * 2 + v // 2) * 4 + (u % 2) * 2 + v % 2
    atom_row = lax.broadcasted_iota(jnp.int32, (128, 128), 0) % 64
    target_row = lax.broadcasted_iota(jnp.int32, (16, 128), 0)
    left, right = [], []
    for r in range(8):
        here = target_row == row_of(target, r)
        stack = [jnp.where(here, row_of(e, r), 0.0) for e in (e_x, e_y, e_z)]
        high = [e.astype(bf16).astype(f32) for e in stack]
        low = [e - h for e, h in zip(stack, high)]
        left.append(jnp.concatenate(high + low, axis=0).astype(bf16))
        right.append(jnp.where(atom_row == row_of(atom, r), 1.0, 0.0).astype(bf16))
    far = lax.dot_general(
        jnp.concatenate(left, axis=1),
        jnp.concatenate(right, axis=1),
        (((1,), (1,)), ((), ())),
        preferred_element_type=f32,
    )
    far = far[:48] + far[48:]
    home = (home_u // 2 * 2 + home_v // 2) * 4 + home_u % 2 * 2 + home_v % 2
    near = [half_turn(jnp.sum(e, axis=0, keepdims=True)) for e in (e_x, e_y, e_z)]
    to_x, to_y, to_z = [
        far[16 * i : 16 * i + 16] - jnp.where(target_row == home, near[i], 0.0) for i in range(3)
    ]
    first = jnp.where(lower, to_x, to_y)
    second = jnp.where(lower, to_z, 0.0)
    for i in range(16):
        row = i % 4 * 2
        grad_ref[i // 4, row : row + 1, :] = first[i : i + 1]
        grad_ref[i // 4, row + 1 : row + 2, :] = second[i : i + 1]


vmem = pl.BlockSpec(memory_space=pltpu.VMEM)


def edges(*operands):
    return pl.pallas_call(
        edge_kernel,
        out_shape=(
            jax.ShapeDtypeStruct((4, 8, 128), f32),
            jax.ShapeDtypeStruct((1, 64), f32),
        ),
        in_specs=[vmem] * len(operands),
        out_specs=(vmem, vmem),
        scratch_shapes=[
            pltpu.VMEM((128, 1024), f32),
            pltpu.VMEM((128, 1024), f32),
            pltpu.VMEM((128, 1024), f32),
            pltpu.VMEM((128, 1024), bf16),
            pltpu.VMEM((64, 1024), f32),
            pltpu.VMEM((64, 1024), f32),
            pltpu.VMEM((9, 64, 128), f32),
            pltpu.VMEM((3, 64, 1024), f32),
            pltpu.VMEM((128, 1024), bf16),
            pltpu.VMEM((64, 1024), bf16),
            pltpu.VMEM((9, 64, 128), f32),
            pltpu.VMEM((19, 8, 128), f32),
            pltpu.VMEM((8, 128), f32),
        ],
        compiler_params=pltpu.CompilerParams(vmem_limit_bytes=16 * 1024 * 1024),
        name="edges",
    )(*operands)


def local(
    positions,
    species,
    charges,
    neighbours,
    counts,
    send_list,
    species_table,
    charge_weight,
    w_center,
    w_neigh,
    w_radial,
    w_two,
    w_env,
    w_tensor,
    w_latent,
    w_out,
):
    first = pl.pallas_call(
        pack_kernel,
        out_shape=jax.ShapeDtypeStruct((4, 8, 128), f32),
        in_specs=[vmem] * 4,
        out_specs=vmem,
        compiler_params=pltpu.CompilerParams(vmem_limit_bytes=1024 * 1024),
        name="pack",
    )(positions.reshape(3, 1, 64), charges[0], species[0], send_list[0])
    second, whole = pl.pallas_call(
        spread_kernel,
        out_shape=(
            jax.ShapeDtypeStruct((4, 32, 128), f32),
            jax.ShapeDtypeStruct((24, 64), jnp.int32),
        ),
        in_specs=[vmem] * 3,
        out_specs=(vmem, vmem),
        compiler_params=pltpu.CompilerParams(vmem_limit_bytes=1024 * 1024),
        name="spread",
    )(swap(first, FORTH[0]).reshape(32, 128), neighbours[0, 0], counts[0])
    grads, energy = edges(
        swap(second, FORTH[1]),
        whole,
        species_table,
        charge_weight[None],
        w_center,
        w_neigh,
        w_radial,
        w_two,
        w_env[0].T,
        w_tensor[0].T,
        w_latent[0],
        w_out[None],
    )
    sums = jnp.sum(swap(grads, BACK[0]), axis=0).reshape(4, 2, 128)
    forces = pl.pallas_call(
        force_kernel,
        out_shape=jax.ShapeDtypeStruct((3, 1, 64), f32),
        in_specs=[vmem],
        out_specs=vmem,
        compiler_params=pltpu.CompilerParams(vmem_limit_bytes=1024 * 1024),
        name="forces",
    )(swap(sums, BACK[1]))
    return (energy[None], forces.reshape(1, 1, 3, 64))


def solution(mesh):
    return jax.shard_map(
        local,
        mesh=mesh,
        in_specs=(
            P("gx", "yz", None, None),
            P("gx", "yz", None),
            P("gx", "yz", None),
            P("gx", "yz", None, None),
            P("gx", "yz", None),
            P("gx", "yz", None),
            P(),
            P(),
            P(),
            P(),
            P(),
            P(),
            P(),
            P(),
            P(),
            P(),
        ),
        out_specs=(P("gx", "yz", None), P("gx", "yz", None, None)),
        check_vma=False,
    )
```

```python
import jax
import jax.numpy as jnp
from jax import lax
from jax.experimental import pallas as pl
from jax.experimental.pallas import tpu as pltpu
from jax.sharding import PartitionSpec as P

box_side = 3.0
f32 = jnp.float32
bf16 = jnp.bfloat16


FORTH = ((0, 0), (1, 1))
BACK = ((0, 0), (1, 1))


def groups_of(pairing):
    slabs, columns = lax.axis_size("gx"), lax.axis_size("yz")
    return [
        [
            (2 * m + pairing[0] + a) % slabs * columns + (2 * n + pairing[1] + b) % columns
            for a in (0, 1)
            for b in (0, 1)
        ]
        for m in range(slabs // 2)
        for n in range(columns // 2)
    ]


def swap(value, pairing):
    return lax.all_to_all(value, ("gx", "yz"), 0, 0, axis_index_groups=groups_of(pairing))


def centre_of(odd, outer):
    return 2 - odd if outer else 1 + odd


def halves(value):
    high = value.astype(bf16).astype(f32)
    return high, value - high


def turned(value):
    return value.astype(f32).T.astype(bf16)


def mm(a, b):
    return jnp.dot(a, b, preferred_element_type=f32)


span = 8


def repeat(value, axis=1):
    return jnp.concatenate([value] * span, axis=axis)


def half_turn(x):
    return x + pltpu.roll(x, 64, 1)


def gate(x):
    half = 0.5 * x
    turn = jnp.tanh(half)
    act = half * turn + half
    return act, 0.5 + 0.5 * (turn + act - act * turn)


def pack_kernel(pos_ref, charge_ref, kind_ref, send_ref, out_ref):
    out_ref[...] = jnp.zeros_like(out_ref)
    code = (kind_ref[:, 0:56] + 8 * send_ref[...]).astype(f32)
    for k in range(4):
        out_ref[k, 0:1, :] = jnp.concatenate([pos_ref[0], pos_ref[1]], axis=1)
        out_ref[k, 1:2, :] = jnp.concatenate([pos_ref[2], charge_ref[...]], axis=1)
        out_ref[k, 2:3, 0:64] = kind_ref[...].astype(f32)
        out_ref[k, 2:3, 0:56] = code


def spread_kernel(four_ref, nb_ref, count_ref, out_ref, whole_ref):
    for k in range(4):
        out_ref[k] = four_ref[...]
    whole_ref[0:16, :] = nb_ref[...]
    whole_ref[16:17, :] = count_ref[...]


def force_kernel(parts_ref, out_ref):
    total = parts_ref[0] + parts_ref[1] + parts_ref[2] + parts_ref[3]
    out_ref[0] = -total[0:1, 0:64]
    out_ref[1] = -pltpu.roll(total, 64, 1)[0:1, 0:64]
    out_ref[2] = -total[1:2, 0:64]


def edge_kernel(
    blocks_ref,
    whole_ref,
    table_ref,
    charge_weight_ref,
    w_center_ref,
    w_neigh_ref,
    w_radial_ref,
    w_two_ref,
    w_env_t_ref,
    w_tensor_t_ref,
    w_latent_ref,
    w_out_ref,
    grad_ref,
    energy_ref,
    lat_ref,
    ds1_ref,
    ds2_ref,
    lb_ref,
    er_ref,
    ch_ref,
    s_ref,
    dg_ref,
    du_ref,
    dch_ref,
    dsum_ref,
    rows_ref,
    table8_ref,
):
    table8_ref[...] = jnp.zeros_like(table8_ref)
    table8_ref[0:6, :] = table_ref[...]
    w_center_t = turned(w_center_ref[...])
    w_neigh_t = turned(w_neigh_ref[...])
    w_two_t = turned(w_two_ref[...])
    w_ec_t = jnp.concatenate([w_env_t_ref[...], w_tensor_t_ref[...]], axis=0)
    w_scal = w_latent_ref[128:320, :]
    w_out = w_out_ref[...].astype(f32)
    w_out_row = jnp.broadcast_to(w_out, (16, 128)).astype(bf16)
    kind_high, rest = halves(table8_ref[...])
    kind_mid, kind_low = halves(rest)
    rad_high, rad_low = halves(w_radial_ref[...])
    none = jnp.zeros((8, 128), f32)
    small = jnp.concatenate(
        [rad_high, rad_low, rad_high, none, kind_high, kind_mid, kind_low, none, jnp.zeros((64, 128), f32)],
        axis=0,
    ).T.astype(bf16)
    w_pair = jnp.concatenate([w_neigh_t, small[:, 0:32]], axis=1)
    w_kind = small[:, 32:64]
    w_rad = jnp.concatenate([rad_high, rad_low], axis=0).astype(bf16)
    cw = jnp.broadcast_to(charge_weight_ref[...], (128, 128)).T

    odd_x = lax.rem(lax.axis_index("gx"), 2)
    odd_y = lax.rem(lax.axis_index("yz"), 2)

    def block(b):
        u = centre_of(odd_x, FORTH[1][0]) + (b // 3 - 1)
        v = centre_of(odd_y, FORTH[1][1]) + (b % 3 - 1)
        far = (u // 2) * 2 + v // 2
        near = (u % 2) * 2 + v % 2
        return [blocks_ref[far, pl.ds(near * 8 + i, 1), :] for i in range(3)]

    tables = [block(b) for b in range(9)]

    ids = jnp.concatenate([whole_ref[0:8, :], whole_ref[8:16, :]], axis=1)
    count = jnp.concatenate([whole_ref[16:17, :], whole_ref[16:17, :]], axis=1)
    row = lax.broadcasted_iota(jnp.int32, (8, 128), 0)
    lane = lax.broadcasted_iota(jnp.int32, (8, 128), 1)
    slot = row + jnp.where(lane >= 64, 8, 0)
    live = jnp.where(slot < count, 1.0, 0.0)
    own = ids < 64
    beyond = ids - 64
    blk = jnp.zeros_like(ids)
    for b in range(1, 9):
        blk = blk + jnp.where(beyond >= 56 * b, 1, 0)
    place = jnp.where(own, ids, beyond - 56 * blk)
    blk = jnp.where(own, 4, blk)

    def pick(which, index, start):
        out = start
        for b in range(9):
            table = jnp.broadcast_to(tables[b][which], (8, 128))
            value = jnp.take_along_axis(table, index, axis=1, mode="promise_in_bounds")
            out = jnp.where(blk == b, value, out)
        return out

    zero = jnp.zeros((8, 128), f32)
    listed = pick(2, place, zero).astype(jnp.int32) // 8
    atom = jnp.where(own, ids, listed)
    far_x = pick(0, atom, zero)
    far_y = pick(0, atom + 64, zero)
    far_z = pick(1, atom, zero)
    far_q = pick(1, atom + 64, zero)
    far_s = (pick(2, atom, zero).astype(jnp.int32) % 8).astype(f32)
    step_x = jnp.where(blk >= 6, 1, jnp.where(blk >= 3, 0, -1))
    step_y = blk - 3 * (step_x + 1) - 1
    lower = lax.broadcasted_iota(jnp.int32, (1, 128), 1) < 64
    mine = [(table, pltpu.roll(table, 64, 1)) for table in tables[4]]
    (own_x, own_y), (own_z, own_q) = [
        (jnp.where(lower, here, there), jnp.where(lower, there, here)) for here, there in mine[:2]
    ]
    own_s = (half_turn(tables[4][2]).astype(jnp.int32) % 8).astype(f32)
    off_x = far_x + box_side * step_x.astype(f32) - own_x
    off_y = far_y + box_side * step_y.astype(f32) - own_y
    off_z = far_z - own_z
    square = off_x * off_x + off_y * off_y + off_z * off_z + 1.0
    dist = jnp.sqrt(square)
    inv = 1.0 / dist
    x, y, z = off_x * inv, off_y * inv, off_z * inv
    harm = [
        None,
        x,
        y,
        z,
        x * y,
        y * z,
        x * z,
        x * x - y * y,
        2.0 * z * z - x * x - y * y,
    ]
    weight = jnp.exp(square * (-1.0 / 32.0)) * live

    kind_row = lax.broadcasted_iota(jnp.int32, (8, 128), 0).astype(f32)
    cw2 = repeat(cw)
    centres = 1.0 + lax.broadcasted_iota(jnp.int32, (8, 128 * span), 0).astype(f32)

    def hidden(kind, charge, wide_cw, wide_row):
        onehot = jnp.where(kind == wide_row, 1.0, 0.0)
        pad = jnp.zeros_like(onehot)
        rhs = jnp.concatenate([onehot, onehot, onehot, pad], axis=0).astype(bf16)
        mixed = mm(w_kind, rhs) + wide_cw * charge
        return gate(mixed)[0]

    center = mm(
        w_center_t, hidden(own_s, own_q, cw, kind_row).astype(bf16)
    )
    center2 = repeat(center)
    kind_row2 = repeat(kind_row)

    def wide(packed, c):
        return jnp.concatenate([packed[r : r + 1, :] for r in range(span * c, span * c + span)], axis=1)

    def basis(c):
        spread = wide(dist, c) - centres
        return spread, jnp.exp(-2.0 * spread * spread)

    for c in range(8 // span):
        at = slice(128 * span * c, 128 * span * (c + 1))
        hid = hidden(wide(far_s, c), wide(far_q, c), cw2, kind_row2)
        _, rb = basis(c)
        rb_high = rb.astype(bf16).astype(f32)
        rhs = jnp.concatenate([hid, rb_high, rb_high, rb - rb_high, jnp.zeros_like(rb)], axis=0)
        pair = mm(w_pair, rhs.astype(bf16)) + center2
        act, ds1_ref[:, at] = gate(pair)
        second = mm(w_two_t, act.astype(bf16))
        latent, ds2_ref[:, at] = gate(second)
        lat_ref[:, at] = latent
        latent_bf = latent.astype(bf16)
        lb_ref[:, at] = latent_bf
        both = mm(w_ec_t, latent_bf)
        er_ref[:, at] = both[:64]
        ch_ref[:, at] = both[64:]

    w_lat_t = jnp.concatenate(
        [turned(w_latent_ref[0:128, :]), turned(w_latent_ref[128:256, :]), turned(w_latent_ref[256:320, :])],
        axis=1,
    )
    w_back = jnp.concatenate([w_latent_ref[0:128, :], turned(w_ec_t)], axis=1)
    wo = jnp.broadcast_to(w_out, (128, 128)).T
    wo2 = repeat(wo)

    def row_of(packed, r):
        return packed[r : r + 1, :]

    def lanes(r):
        return slice(128 * r, 128 * r + 128)

    group_of = [0, 1, 1, 1, 2, 2, 2, 2, 2]
    weighted = [None] + [h * weight for h in harm[1:]]
    for m in range(9):
        scale = weight if m == 0 else weighted[m]
        total = er_ref[:, lanes(0)] * row_of(scale, 0)
        for r in range(1, 8):
            total = total + er_ref[:, lanes(r)] * row_of(scale, r)
        s_ref[m] = 0.25 * half_turn(total)

    def keep_row(index, c, value):
        for i in range(span):
            rows_ref[index, span * c + i : span * c + i + 1, :] = value[:, 128 * i : 128 * i + 128]

    for c in range(8 // span):
        at = slice(128 * span * c, 128 * span * (c + 1))
        channel = ch_ref[:, at]
        grouped = [repeat(s_ref[0]), None, None]
        for m in range(1, 9):
            term = repeat(s_ref[m]) * wide(harm[m], c)
            g = group_of[m]
            grouped[g] = term if grouped[g] is None else grouped[g] + term
        scalars = [(g * channel).astype(bf16) for g in grouped]
        joined = jnp.concatenate([lb_ref[:, at]] + scalars, axis=0)
        update = mm(w_lat_t, joined)
        act, slope = gate(update)
        out_bf = (lat_ref[:, at] + act).astype(bf16)
        keep_row(0, c, mm(w_out_row, out_bf)[0:1])
        d_update = (wo2 * wide(weight, c) * slope).astype(bf16)
        du_ref[:, at] = d_update
        d_scal = mm(w_scal, d_update)
        d_grouped = []
        d_channel = None
        for g in range(3):
            part = d_scal[64 * g : 64 * g + 64]
            term = part * grouped[g]
            d_channel = term if d_channel is None else d_channel + term
            d_grouped.append(part * channel)
            dg_ref[g, :, at] = d_grouped[g]
        dch_ref[:, at] = d_channel.astype(bf16)
        for m in range(1, 9):
            keep_row(m, c, jnp.sum(d_grouped[group_of[m]] * repeat(s_ref[m]), axis=0, keepdims=True))

    for m in range(9):
        g = group_of[m]
        total = None
        for r in range(8):
            term = dg_ref[g, :, lanes(r)]
            if m > 0:
                term = term * row_of(harm[m], r)
            total = term if total is None else total + term
        dsum_ref[m] = 0.25 * half_turn(total)

    for c in range(8 // span):
        at = slice(128 * span * c, 128 * span * (c + 1))
        raw = er_ref[:, at]
        w_row = wide(weight, c)
        d_env = repeat(dsum_ref[0])
        for m in range(1, 9):
            back = repeat(dsum_ref[m])
            d_env = d_env + back * wide(harm[m], c)
            keep_row(8 + m, c, jnp.sum(raw * back, axis=0, keepdims=True))
        keep_row(17, c, jnp.sum(raw * d_env, axis=0, keepdims=True))
        d_joined = jnp.concatenate(
            [du_ref[:, at], (d_env * w_row).astype(bf16), dch_ref[:, at]], axis=0
        )
        d_latent = mm(w_back, d_joined) + wo2 * w_row
        d_second = (d_latent * ds2_ref[:, at]).astype(bf16)
        d_pair = mm(w_two_ref[...], d_second) * ds1_ref[:, at]
        high = d_pair.astype(bf16)
        low = (d_pair - high.astype(f32)).astype(bf16)
        first = mm(w_rad, high)
        d_basis = first[0:8] + first[8:16] + mm(w_rad, low)[0:8]
        spread, rb = basis(c)
        keep_row(18, c, jnp.sum(d_basis * rb * spread, axis=0, keepdims=True) * -4.0)

    energy = jnp.sum(rows_ref[0] * weight, axis=0, keepdims=True)
    energy_ref[...] = half_turn(energy)[:, :64]
    d_h = [None] + [rows_ref[m] + weight * rows_ref[8 + m] for m in range(1, 9)]
    g_x = d_h[1] + y * d_h[4] + z * d_h[6] + 2.0 * x * (d_h[7] - d_h[8])
    g_y = d_h[2] + x * d_h[4] + z * d_h[5] - 2.0 * y * (d_h[7] + d_h[8])
    g_z = d_h[3] + y * d_h[5] + x * d_h[6] + 4.0 * z * d_h[8]
    d_weight = rows_ref[0] + rows_ref[17]
    d_dist = (
        rows_ref[18]
        - inv * (g_x * x + g_y * y + g_z * z)
        - d_weight * weight * dist * (1.0 / 16.0)
    )
    e_x = g_x * inv + d_dist * x
    e_y = g_y * inv + d_dist * y
    e_z = g_z * inv + d_dist * z

    home_u = centre_of(odd_x, BACK[0][0])
    home_v = centre_of(odd_y, BACK[0][1])
    u = home_u + step_x
    v = home_v + step_y
    target = ((u // 2) * 2 + v // 2) * 4 + (u % 2) * 2 + v % 2
    atom_row = lax.broadcasted_iota(jnp.int32, (128, 128), 0) % 64
    target_row = lax.broadcasted_iota(jnp.int32, (16, 128), 0)
    left, right = [], []
    for r in range(8):
        here = target_row == row_of(target, r)
        stack = [jnp.where(here, row_of(e, r), 0.0) for e in (e_x, e_y, e_z)]
        high = [e.astype(bf16).astype(f32) for e in stack]
        low = [e - h for e, h in zip(stack, high)]
        left.append(jnp.concatenate(high + low, axis=0).astype(bf16))
        right.append(jnp.where(atom_row == row_of(atom, r), 1.0, 0.0).astype(bf16))
    far = lax.dot_general(
        jnp.concatenate(left, axis=1),
        jnp.concatenate(right, axis=1),
        (((1,), (1,)), ((), ())),
        preferred_element_type=f32,
    )
    far = far[:48] + far[48:]
    home = (home_u // 2 * 2 + home_v // 2) * 4 + home_u % 2 * 2 + home_v % 2
    near = [half_turn(jnp.sum(e, axis=0, keepdims=True)) for e in (e_x, e_y, e_z)]
    to_x, to_y, to_z = [
        far[16 * i : 16 * i + 16] - jnp.where(target_row == home, near[i], 0.0) for i in range(3)
    ]
    first = jnp.where(lower, to_x, to_y)
    second = jnp.where(lower, to_z, 0.0)
    for i in range(16):
        row = i % 4 * 2
        grad_ref[i // 4, row : row + 1, :] = first[i : i + 1]
        grad_ref[i // 4, row + 1 : row + 2, :] = second[i : i + 1]


vmem = pl.BlockSpec(memory_space=pltpu.VMEM)


def edges(*operands):
    return pl.pallas_call(
        edge_kernel,
        out_shape=(
            jax.ShapeDtypeStruct((4, 8, 128), f32),
            jax.ShapeDtypeStruct((1, 64), f32),
        ),
        in_specs=[vmem] * len(operands),
        out_specs=(vmem, vmem),
        scratch_shapes=[
            pltpu.VMEM((128, 1024), f32),
            pltpu.VMEM((128, 1024), f32),
            pltpu.VMEM((128, 1024), f32),
            pltpu.VMEM((128, 1024), bf16),
            pltpu.VMEM((64, 1024), f32),
            pltpu.VMEM((64, 1024), f32),
            pltpu.VMEM((9, 64, 128), f32),
            pltpu.VMEM((3, 64, 1024), f32),
            pltpu.VMEM((128, 1024), bf16),
            pltpu.VMEM((64, 1024), bf16),
            pltpu.VMEM((9, 64, 128), f32),
            pltpu.VMEM((19, 8, 128), f32),
            pltpu.VMEM((8, 128), f32),
        ],
        compiler_params=pltpu.CompilerParams(vmem_limit_bytes=16 * 1024 * 1024),
        name="edges",
    )(*operands)


def local(
    positions,
    species,
    charges,
    neighbours,
    counts,
    send_list,
    species_table,
    charge_weight,
    w_center,
    w_neigh,
    w_radial,
    w_two,
    w_env,
    w_tensor,
    w_latent,
    w_out,
):
    first = pl.pallas_call(
        pack_kernel,
        out_shape=jax.ShapeDtypeStruct((4, 8, 128), f32),
        in_specs=[vmem] * 4,
        out_specs=vmem,
        compiler_params=pltpu.CompilerParams(vmem_limit_bytes=1024 * 1024),
        name="pack",
    )(positions.reshape(3, 1, 64), charges[0], species[0], send_list[0])
    second, whole = pl.pallas_call(
        spread_kernel,
        out_shape=(
            jax.ShapeDtypeStruct((4, 32, 128), f32),
            jax.ShapeDtypeStruct((24, 64), jnp.int32),
        ),
        in_specs=[vmem] * 3,
        out_specs=(vmem, vmem),
        compiler_params=pltpu.CompilerParams(vmem_limit_bytes=1024 * 1024),
        name="spread",
    )(swap(first, FORTH[0]).reshape(32, 128), neighbours[0, 0], counts[0])
    grads, energy = edges(
        swap(second, FORTH[1]),
        whole,
        species_table,
        charge_weight[None],
        w_center,
        w_neigh,
        w_radial,
        w_two,
        w_env[0].T,
        w_tensor[0].T,
        w_latent[0],
        w_out[None],
    )
    sums = jnp.sum(swap(grads, BACK[0]), axis=0).reshape(4, 2, 128)
    forces = pl.pallas_call(
        force_kernel,
        out_shape=jax.ShapeDtypeStruct((3, 1, 64), f32),
        in_specs=[vmem],
        out_specs=vmem,
        compiler_params=pltpu.CompilerParams(vmem_limit_bytes=1024 * 1024),
        name="forces",
    )(swap(sums, BACK[1]))
    return (energy[None], forces.reshape(1, 1, 3, 64))


def solution(mesh):
    return jax.shard_map(
        local,
        mesh=mesh,
        in_specs=(
            P("gx", "yz", None, None),
            P("gx", "yz", None),
            P("gx", "yz", None),
            P("gx", "yz", None, None),
            P("gx", "yz", None),
            P("gx", "yz", None),
            P(),
            P(),
            P(),
            P(),
            P(),
            P(),
            P(),
            P(),
            P(),
            P(),
        ),
        out_specs=(P("gx", "yz", None), P("gx", "yz", None, None)),
        check_vma=False,
    )
```
